256 devices in a mesh: field: 32 (over z, x_hi, core), row: 8 (over y, x_lo).
Axes of the slice: x: 4 (x_hi: 2, x_lo: 2; x = x_hi * 2 + x_lo), y: 4, z: 8, core: 2. Of those that a mesh axis runs over, the one named last changes fastest.
Arguments:
- direction: bfloat16 [32, 2, 512, 512], P('field', None, 'row'), may hold values from -6 to 6
- slits: int32 [64], P('field'), may hold values from 0 to 511
- sources: int32 [4], replicated, may hold values from 0 to 80
- support: int32 [512, 512], P('row'), may hold values from 0 to 1, as said below
- focus: float32 [3], replicated, may hold values from -2 to 2
- slit_focus: float32 [64], P('field'), may hold values from -1.5 to 1.5
- obj_rows: float32 [2, 576], replicated, may hold values from -6 to 6
- obj_cols: float32 [2, 576], replicated, may hold values from -6 to 6
- weights: float32 [4, 3, 128, 128], replicated, may hold values from 0.25 to 4
Outputs:
- curvature_product: float32 [32, 2, 512, 512], P('field', None, 'row')
The draws below stay inside these ranges and needn't reach their ends.
Inputs may be any that keep to these rules, and one draw needn't show every extreme that they name: `support`: 1 where the pupil transmits, 0 elsewhere.
All inputs are finite; a program needn't handle non-finite values.
Results may differ from the reference program's by a relative error of at most 0.0022.
Values may be sent and summed in bfloat16 or wider, within the bound.
A program may use at most 192 MiB of HBM per device.

```python
import math
import jax
import jax.numpy as jnp
from jax import lax

N = 512
K = 8
J = 4
M = 128
Z = 3
SRC = 4
SLIT_GRID = 512
SRC_SIDE = 9
SHIFT = 8
PAD = 32
SLITS = 64


def draw_support(key, part):
    key = jax.random.fold_in(key, 11)
    outer_key, inner_key, defect_key = jax.random.split(key, 3)
    outer = jax.random.randint(outer_key, (), 3 * N // 8, N // 2 + 1)
    inner = jax.random.randint(inner_key, (), N // 16, N // 8 + 1)
    grid = 2 * jnp.arange(N, dtype=jnp.int32) - N + 1
    radius = grid[:, None] * grid[:, None] + grid[None, :] * grid[None, :]
    inside = (radius <= 4 * outer * outer) & (radius >= 4 * inner * inner)
    intact = jax.random.randint(defect_key, (N, N), 0, 16) > 0
    return (inside & intact).astype(jnp.int32)


def place_ends(drawn, key, smallest, top_value):
    longest = drawn.shape.index(max(drawn.shape))
    spots = []
    for shift in (0, 1):
        where = [jax.random.randint(jax.random.fold_in(key, axis), (), 0, length) for axis, length in enumerate(drawn.shape)]
        where[longest] = (where[longest] + shift) % drawn.shape[longest]
        spots.append(tuple(where))
    return drawn.at[spots[0]].set(smallest).at[spots[1]].set(top_value)


def level_of(rng, shape, pieces, smallest, largest):
    factor_of, own = 1.0, jax.random.fold_in(rng, 6)
    for dim, parts in pieces:
        heights = jnp.exp(jax.random.uniform(jax.random.fold_in(own, dim), (parts,), jnp.float32, smallest / len(pieces), largest / len(pieces)))
        factor_of = factor_of * jnp.repeat(heights, shape[dim] // parts).reshape([-1 if axis == dim else 1 for axis in range(len(shape))])
    return factor_of


def scatter_about(own_key, extent, width, limit, cuts=(), kind=jnp.bfloat16):
    gain = level_of(own_key, extent, cuts, -0.22, 0.18) if cuts else 1.0
    result = jax.random.normal(own_key, extent, jnp.float32) * width * gain
    return jnp.minimum(jnp.maximum(result, -limit), limit).astype(kind)


def setup_inputs(seed: int = 0) -> dict:
    keys = jax.random.split(jax.random.key(seed), 10)
    return {
        "direction": scatter_about(keys[0], (K * J, 2, N, N), 1.0, 6.0, ((0, 32), (2, 8))),
        "slits": place_ends(jax.random.randint(keys[1], (SLITS,), 0, SLIT_GRID), jax.random.fold_in(keys[1], 1), 0, SLIT_GRID - 1).astype(jnp.int32),
        "sources": place_ends(jax.random.randint(keys[2], (SRC,), 0, SRC_SIDE * SRC_SIDE), jax.random.fold_in(keys[2], 1), 0, (SRC_SIDE * SRC_SIDE) - 1).astype(jnp.int32),
        "support": draw_support(jax.random.fold_in(keys[9], 71), 0),
        "focus": jnp.clip(jax.random.uniform(keys[4], (Z,), jnp.float32, -2.0, 2.0), -2.0, 2.0),
        "slit_focus": jnp.clip(jax.random.uniform(keys[5], (SLITS,), jnp.float32, -1.5, 1.5) * level_of(keys[5], (SLITS,), ((0, 32),), -0.4, 0.0), -1.5, 1.5),
        "obj_rows": scatter_about(keys[6], (2, N + 2 * PAD), 1.0, 6.0, (), jnp.float32),
        "obj_cols": scatter_about(keys[7], (2, N + 2 * PAD), 1.0, 6.0, (), jnp.float32),
        "weights": jnp.clip(jnp.exp(jax.random.uniform(keys[8], (SRC, Z, M, M), jnp.float32, math.log(0.25), math.log(4.0))), 0.25, 4.0),
    }


def legendre(slits):
    position = (2.0 * slits.astype(jnp.float32) + 1.0) / SLIT_GRID - 1.0
    values = [jnp.ones_like(position), position]
    for order in range(1, K - 1):
        values.append(((2.0 * order + 1.0) * position * values[order] - order * values[order - 1]) / (order + 1.0))
    return jnp.stack(values[:K], axis=1)

def tables(sources, defocus, obj_rows, obj_cols):
    freq = jnp.arange(N, dtype=jnp.int32)
    radial = ((2 * freq - N + 1).astype(jnp.float32) / N) ** 2
    theta = math.pi * defocus[:, :, None] * radial[None, None, :]
    turn_cos = jnp.cos(theta)
    turn_sin = jnp.sin(theta)
    middle = SRC_SIDE // 2
    row_shift = (SHIFT * (sources // SRC_SIDE - middle)).astype(jnp.int32)
    col_shift = (SHIFT * (sources % SRC_SIDE - middle)).astype(jnp.int32)

    def window(spectrum, offset):
        return lax.dynamic_slice_in_dim(spectrum, (PAD - offset).astype(jnp.int32), N, 1)

    def factor(spectrum, offsets):
        picked = jax.vmap(window, in_axes=(None, 0))(spectrum, offsets)
        first = picked[None, :, None, 0, :]
        second = picked[None, :, None, 1, :]
        real_part = first * turn_cos[:, None] - second * turn_sin[:, None]
        imag_part = first * turn_sin[:, None] + second * turn_cos[:, None]
        return (real_part, imag_part)

    def kernel(stretch):
        centered = (freq - N // 2)[:, None] * (jnp.arange(M, dtype=jnp.int32) - M // 2)[None, :]
        angle = jnp.mod(stretch * centered, N).astype(jnp.float32) * (-2.0 * math.pi / N)
        scale = 1.0 / math.sqrt(M)
        return (jnp.cos(angle) * scale, jnp.sin(angle) * scale)

    def apply(fac_re, fac_im, ker_re, ker_im):
        real_part = fac_re[..., None] * ker_re - fac_im[..., None] * ker_im
        imag_part = fac_re[..., None] * ker_im + fac_im[..., None] * ker_re
        return (real_part.astype(jnp.bfloat16), imag_part.astype(jnp.bfloat16))
    col_re, col_im = factor(obj_cols, col_shift)
    ker_re, ker_im = kernel(1)
    map_re, map_im = apply(col_re, col_im, ker_re, ker_im)
    upper = jnp.stack([map_re, map_im], axis=4)
    lower = jnp.stack([-map_im, map_re], axis=4)
    block = jnp.stack([upper, lower], axis=3)
    block = block.reshape(block.shape[0], block.shape[1], block.shape[2], 2 * N, 2 * M)
    row_re, row_im = factor(obj_rows, row_shift)
    ker_re, ker_im = kernel(2)
    rows_re, rows_im = apply(row_re, row_im, ker_re, ker_im)
    return (block, rows_re, rows_im)

def rounded(values):
    return lax.optimization_barrier(values.astype(jnp.bfloat16)).astype(jnp.float32)

def reference(direction, slits, sources, support, focus, slit_focus, obj_rows, obj_cols, weights):
    basis = legendre(slits).astype(jnp.bfloat16)
    coeffs = direction.reshape(K, J, 2, N, N).astype(jnp.float32)
    mask = support.astype(jnp.float32)
    src_count = sources.shape[0]
    plane_count = focus.shape[0]

    def one_slit(running, inputs):
        basis_row, own_focus = inputs
        defocus = (focus + own_focus)[None, :]
        block, rows_re, rows_im = tables(sources, defocus, obj_rows, obj_cols)
        block = block[0].astype(jnp.float32)
        rows_re = rows_re[0].astype(jnp.float32)
        rows_im = rows_im[0].astype(jnp.float32)
        weight_row = basis_row.astype(jnp.float32)
        pupil = jnp.einsum('k,kjcrn->jrcn', weight_row, coeffs) * mask[None, :, None, :]
        pupil = rounded(pupil).reshape(J, N, 2 * N)
        spectra = rounded(jnp.einsum('jrc,qzcy->jqzry', pupil, block))
        shape = (J, src_count, plane_count, M, 2, M)
        second = jnp.einsum('qzno,jqzny->jqzoy', rows_im, spectra).reshape(shape)
        primary = jnp.einsum('qzno,jqzny->jqzoy', rows_re, spectra).reshape(shape)
        image_re = primary[..., 0, :] - second[..., 1, :]
        image_im = primary[..., 1, :] + second[..., 0, :]
        scaled = jnp.stack([weights[None] * image_re, weights[None] * image_im], axis=4)
        scaled = rounded(scaled.reshape(J, src_count, plane_count, M, 2 * M))
        shape = (J, src_count, plane_count, N, 2, M)
        back_one = jnp.einsum('qzno,jqzoy->jqzny', rows_re, scaled).reshape(shape)
        back_two = jnp.einsum('qzno,jqzoy->jqzny', rows_im, scaled).reshape(shape)
        adjoint = jnp.stack([back_one[..., 0, :] + back_two[..., 1, :], back_one[..., 1, :] - back_two[..., 0, :]], axis=4)
        adjoint = rounded(adjoint.reshape(J, src_count, plane_count, N, 2 * M))
        pulled = jnp.einsum('jqzry,qzcy->jrc', adjoint, block).reshape(J, N, 2, N)
        pulled = rounded(pulled * mask[None, :, None, :])
        return (running + jnp.einsum('k,jrcn->kjcrn', weight_row, pulled), None)
    start = jnp.zeros((K, J, 2, N, N), jnp.float32)
    running, _ = lax.scan(one_slit, start, (basis, slit_focus))
    factor = 4.0 / (src_count * plane_count * SLITS)
    return (running * factor).reshape(K * J, 2, N, N)
```

```python
import functools
import math

import jax
import jax.numpy as jnp
import numpy as np
from jax import lax
from jax.experimental import pallas as pl
from jax.experimental.pallas import tpu as pltpu
from jax.sharding import PartitionSpec as P

J = 4
M = 128
SLIT_GRID = 512
SRC_SIDE = 9
SHIFT = 8
PAD = 32
GROUPS = 4
MESH = pl.DeviceIdType.MESH
NT = (((1,), (1,)), ((), ()))


def kernel_tables(size, blocks, groups):
    freq = np.arange(size)
    span = size // (blocks * groups)
    order = freq.reshape(blocks, groups, span).transpose(1, 0, 2).reshape(-1)

    def kernel(stretch):
        turns = np.mod(stretch * (freq - size // 2)[:, None] * (np.arange(M) - M // 2)[None, :], size)
        angle = (turns.astype(np.float32) * np.float32(-2.0 * math.pi / size)).astype(np.float64)
        scale = 1.0 / math.sqrt(M)
        return np.stack([np.cos(angle) * scale, np.sin(angle) * scale]).astype(np.float32)

    cols = np.ascontiguousarray(kernel(1).transpose(0, 2, 1))
    rows = np.ascontiguousarray(kernel(2)[:, order])
    return cols, np.ascontiguousarray(rows.transpose(0, 2, 1)), rows


def body(sizes, slits, sources, focus, slit_focus, direction, support, obj_rows, obj_cols, weights,
         cols_t_hbm, rows_t_hbm, rows_hbm, out,
         cols_t, rows_t, rows, wts, info, coeff, mix, mix_t, fac, fac_t, fac_p, block_t, row_t, row_n,
         pupil_out, pupil_in, image, adjoint, pulled, returned, part, partial_in,
         load_sem, info_send, info_recv, ag_send, ag_recv, out_send, out_recv, back_send, back_recv, rs_send, rs_recv):
    ring, row_count, src_count, plane_count, size, total_slits = sizes
    groups = GROUPS
    span = size // (row_count * groups)
    slab = span * row_count
    bands = src_count * plane_count
    half = ring // 2
    me_f, me_r = lax.axis_index("field"), lax.axis_index("row")
    z, j = me_f // J, me_f % J
    y, x = me_r // 2, me_r % 2
    y_count = row_count // 2
    right = (((z + 1) % ring) * J + j, me_r)
    left = (((z + ring - 1) % ring) * J + j, me_r)
    siblings = [(z * J + (j + d) % J, me_r) for d in range(1, J)]
    steps = [(dy, dx) for dy in (2, 1, 3, 0) for dx in (1, 0) if dy < y_count and (dy, dx) != (0, 0)]
    peers = [((y + dy) % y_count) * 2 + (x + dx) % 2 for dy, dx in steps]

    loads = [
        pltpu.make_async_copy(src, dst, load_sem.at[i])
        for i, (src, dst) in enumerate(
            [(cols_t_hbm, cols_t), (rows_t_hbm, rows_t), (rows_hbm, rows), (weights, wts)]
        )
    ]
    for load in loads:
        load.start()

    barrier = pltpu.get_barrier_semaphore()
    greeted = [right, left] + siblings + [(me_f, peer) for peer in peers]
    for device in greeted:
        pl.semaphore_signal(barrier, inc=1, device_id=device, device_id_type=MESH)

    for g in range(groups):
        mask = support[g * span : (g + 1) * span, :].astype(jnp.float32)
        for c in range(2):
            own = direction[0, c, g * span : (g + 1) * span, :].astype(jnp.float32) * mask
            coeff[g, pl.ds(z * span, span), c * size : (c + 1) * size] = own.astype(jnp.bfloat16)
    for i in range(2):
        position = (2.0 * slits[i].astype(jnp.float32) + 1.0) / SLIT_GRID - 1.0
        info[j, i * span : (i + 1) * span, :] = jnp.full((span, 128), position, jnp.float32)
        info[j, (2 + i) * span : (3 + i) * span, :] = jnp.full((span, 128), slit_focus[i], jnp.float32)

    pl.semaphore_wait(barrier, len(greeted))

    sent = []

    def send(src, dst, send_sem, recv_sem, device):
        copy = pltpu.make_async_remote_copy(
            src_ref=src, dst_ref=dst, send_sem=send_sem, recv_sem=recv_sem, device_id=device, device_id_type=MESH
        )
        copy.start()
        sent.append(copy)

    def arrived(dst, send_sem, recv_sem, device):
        pltpu.make_async_remote_copy(
            src_ref=dst, dst_ref=dst, send_sem=send_sem, recv_sem=recv_sem, device_id=device, device_id_type=MESH
        ).wait_recv()

    def hops(way, g):
        return half if way == g % 2 else half - 1

    def ring_to(way):
        return right if way == 0 else left

    def gather_slot(way, g, h):
        k = (z + ring - h) % ring if way == 0 else (z + h) % ring
        return coeff.at[g, pl.ds(pl.multiple_of(k * span, span), span), :]

    def gather_send(way, g, h):
        slot = gather_slot(way, g, h)
        send(slot, slot, ag_send.at[way, g, h], ag_recv.at[way, g, h], ring_to(way))

    def gather_arrived(way, g, h):
        arrived(gather_slot(way, g, h + 1), ag_send.at[way, g, h], ag_recv.at[way, g, h], ring_to(way))

    for d, device in enumerate(siblings):
        send(info.at[j], info.at[j], info_send.at[d], info_recv.at[d], device)
    for g in range(groups):
        for way in range(2):
            gather_send(way, g, 0)

    for d, device in enumerate(siblings):
        source = (j + J - 1 - d) % J
        arrived(info.at[source], info_send.at[d], info_recv.at[d], device)
    own_focus = info[me_r // 2, pl.ds((2 + me_r % 2) * span, 8), :]
    own_focus = jnp.concatenate([own_focus] * (size // 128), axis=1)
    which = lax.broadcasted_iota(jnp.int32, (8, size), 0)
    plane = jnp.full((8, size), focus[0], jnp.float32)
    for p in range(1, plane_count):
        plane = jnp.where(which == p, focus[p], plane)
    freq = lax.broadcasted_iota(jnp.int32, (8, size), 1)
    scaled = (2 * freq - size + 1).astype(jnp.float32) / size
    theta = math.pi * (plane + own_focus) * (scaled * scaled)
    turn_cos, turn_sin = jnp.cos(theta), jnp.sin(theta)
    middle = SRC_SIDE // 2
    for q in range(src_count):
        for base, spectrum, place in ((0, obj_rows, sources[q] // SRC_SIDE), (64, obj_cols, sources[q] % SRC_SIDE)):
            picked = spectrum[:, PAD + SHIFT * middle : PAD + SHIFT * middle + size]
            for v in range(1, SRC_SIDE):
                start = PAD - SHIFT * (v - middle)
                picked = jnp.where(place == v, spectrum[:, start : start + size], picked)
            first, second = picked[0:1], picked[1:2]
            fac[base + 8 * q : base + 8 * q + 8, :] = first * turn_cos - second * turn_sin
            fac[base + 32 + 8 * q : base + 40 + 8 * q, :] = first * turn_sin + second * turn_cos
    turned = fac[...].T
    for g in range(groups):
        for r in range(row_count):
            start = r * groups * span + g * span
            fac_t[g * slab + r * span : g * slab + (r + 1) * span, :] = turned[start : start + span, :]
    fac_p[...] = fac_t[...].T

    edge = row_count * span
    position = jnp.concatenate([info[s, 0 : 2 * span, :] for s in range(J)], axis=0)
    position = jnp.concatenate([position] * (edge // 128), axis=1) if edge > 128 else position
    sub = lax.broadcasted_iota(jnp.int32, (edge, edge), 0)
    lane = lax.broadcasted_iota(jnp.int32, (edge, edge), 1)
    before, now = jnp.ones_like(position), position
    chosen = jnp.where(lane // span == 0, before, jnp.where(lane // span == 1, now, 0.0))
    for order in range(1, ring - 1):
        before, now = now, ((2.0 * order + 1.0) * position * now - order * before) / (order + 1.0)
        chosen = jnp.where(lane // span == order + 1, now, chosen)
    chosen = jnp.where(sub % span == lane % span, chosen, 0.0)
    mix[...] = chosen.astype(jnp.bfloat16)
    mix_t[...] = chosen.T.astype(jnp.bfloat16)

    for load in loads:
        load.wait()

    def build_lanes(band, carry):
        index = (band // plane_count) * 8 + band % plane_count
        cf_re, cf_im = fac[pl.ds(64 + index, 1), :], fac[pl.ds(96 + index, 1), :]
        rf_re, rf_im = fac_p[pl.ds(index, 1), :], fac_p[pl.ds(32 + index, 1), :]
        base = pl.multiple_of(band * 2 * M, 2 * M)
        for m in range(0, M, 16):
            ker_re, ker_im = cols_t[0, m : m + 16, :], cols_t[1, m : m + 16, :]
            real = (cf_re * ker_re - cf_im * ker_im).astype(jnp.bfloat16)
            imag = (cf_re * ker_im + cf_im * ker_re).astype(jnp.bfloat16)
            block_t[pl.ds(base + m, 16), 0:size] = real
            block_t[pl.ds(base + m, 16), size : 2 * size] = -imag
            block_t[pl.ds(base + M + m, 16), 0:size] = imag
            block_t[pl.ds(base + M + m, 16), size : 2 * size] = real
            ker_re, ker_im = rows_t[0, m : m + 16, :], rows_t[1, m : m + 16, :]
            row_t[pl.ds(base + m, 16), :] = (rf_re * ker_re - rf_im * ker_im).astype(jnp.bfloat16)
            row_t[pl.ds(base + M + m, 16), :] = (rf_re * ker_im + rf_im * ker_re).astype(jnp.bfloat16)
        return carry

    def build_sublanes(step, carry):
        start = pl.multiple_of(step * 32, 32)
        ker_re, ker_im = rows[0, pl.ds(start, 32), :], rows[1, pl.ds(start, 32), :]
        held = fac_t[pl.ds(start, 32), :]
        for band in range(bands):
            index = (band // plane_count) * 8 + band % plane_count
            f_re, f_im = held[:, index : index + 1], held[:, 32 + index : 33 + index]
            row_n[band, pl.ds(start, 32), 0:M] = (f_re * ker_re - f_im * ker_im).astype(jnp.bfloat16)
            row_n[band, pl.ds(start, 32), M : 2 * M] = (f_re * ker_im + f_im * ker_re).astype(jnp.bfloat16)
        return carry

    slots = (half - 1) * groups
    done = 0
    for h in range(1, half):
        for g in range(groups):
            for way in range(2):
                if h <= hops(way, g):
                    gather_arrived(way, g, h - 1)
                    if h < hops(way, g):
                        gather_send(way, g, h)
            upto = ((h - 1) * groups + g + 1) * bands // slots
            if upto > done:
                lax.fori_loop(done, upto, build_lanes, 0)
                done = upto

    for g in range(groups):
        for way in range(2):
            if hops(way, g) == half:
                gather_arrived(way, g, half - 1)
        pupil_out[g] = jnp.dot(mix[...], coeff[g], preferred_element_type=jnp.float32).astype(jnp.bfloat16)
        mine = pl.ds(pl.multiple_of(me_r * span, span), span)
        for d, peer in enumerate(peers):
            theirs = pl.ds(pl.multiple_of(peer * span, span), span)
            send(pupil_out.at[g, theirs, :], pupil_in.at[g, mine, :], out_send.at[d, g], out_recv.at[d, g], (me_f, peer))
        pupil_in[g, mine, :] = pupil_out[g, mine, :]

    lax.fori_loop(0, size // 32, build_sublanes, 0)

    def source_of(d):
        dy, dx = steps[d]
        return ((y + y_count - dy) % y_count) * 2 + (x + 2 - dx) % 2

    for g in range(groups):
        for d in range(len(peers)):
            theirs = pl.ds(pl.multiple_of(source_of(d) * span, span), span)
            arrived(pupil_in.at[g, theirs, :], out_send.at[d, g], out_recv.at[d, g], (me_f, peers[d]))

        def forward(band, carry):
            base = pl.multiple_of(band * 2 * M, 2 * M)
            spectra = lax.dot_general(
                pupil_in[g], block_t[pl.ds(base, 2 * M), :], NT, preferred_element_type=jnp.float32
            ).astype(jnp.bfloat16)
            term = jnp.dot(
                row_t[pl.ds(base, 2 * M), g * slab : (g + 1) * slab], spectra, preferred_element_type=jnp.float32
            )
            image[band] = term if g == 0 else image[band] + term
            return carry

        lax.fori_loop(0, bands, forward, 0)

    def middle_step(band, carry):
        term = image[band]
        weight = wts[band]
        real = (weight * (term[:M, :M] - term[M:, M:])).astype(jnp.bfloat16)
        imag = (weight * (term[:M, M:] + term[M:, :M])).astype(jnp.bfloat16)
        square = jnp.concatenate(
            [jnp.concatenate([real, imag], axis=1), jnp.concatenate([imag, -real], axis=1)], axis=0
        )
        adjoint[:, pl.ds(pl.multiple_of(band * 2 * M, 2 * M), 2 * M)] = jnp.dot(
            row_n[band], square, preferred_element_type=jnp.float32
        ).astype(jnp.bfloat16)
        return carry

    lax.fori_loop(0, bands, middle_step, 0)

    def pull(g):
        def column(tile, carry):
            at = pl.ds(pl.multiple_of(tile * 256, 256), 256)
            pulled[g, :, at] = jnp.dot(
                adjoint[g * slab : (g + 1) * slab, :], block_t[:, at], preferred_element_type=jnp.float32
            ).astype(jnp.bfloat16)
            return carry

        lax.fori_loop(0, 2 * size // 256, column, 0)
        mine = pl.ds(pl.multiple_of(me_r * span, span), span)
        for d, peer in enumerate(peers):
            theirs = pl.ds(pl.multiple_of(peer * span, span), span)
            send(pulled.at[g, theirs, :], returned.at[g, mine, :], back_send.at[d, g], back_recv.at[d, g], (me_f, peer))
        returned[g, mine, :] = pulled[g, mine, :]

    def target(way, g, t):
        away = hops(way, g) - t
        return (z + away) % ring if way == 0 else (z + ring - away) % ring

    def rows_of(k):
        return pl.ds(pl.multiple_of(k * span, span), span)

    def scatter_slot(way, g, t, k):
        if way == 1 and t == hops(way, g) - 1:
            return partial_in.at[g, ring * span : (ring + 1) * span, :]
        return partial_in.at[g, rows_of(k), :]

    def scatter_send(way, g, t):
        k = target(way, g, t)
        send(
            part.at[g, rows_of(k), :], scatter_slot(way, g, t, k),
            rs_send.at[way, g, t], rs_recv.at[way, g, t], ring_to(way),
        )

    def scatter_arrived(way, g, t):
        k = target(way, g, t + 1) if t + 1 < hops(way, g) else z
        slot = scatter_slot(way, g, t, k)
        arrived(slot, rs_send.at[way, g, t], rs_recv.at[way, g, t], ring_to(way))
        return k

    def collect(g):
        for d in range(len(peers)):
            theirs = rows_of(source_of(d))
            arrived(returned.at[g, theirs, :], back_send.at[d, g], back_recv.at[d, g], (me_f, peers[d]))
        part[g] = jnp.dot(mix_t[...], returned[g], preferred_element_type=jnp.float32)
        for way in range(2):
            scatter_send(way, g, 0)

    def advance(g, t):
        for way in range(2):
            if t < hops(way, g):
                k = scatter_arrived(way, g, t - 1)
                part[g, rows_of(k), :] = part[g, rows_of(k), :] + partial_in[g, rows_of(k), :]
                scatter_send(way, g, t)

    factor = 4.0 / (bands * total_slits)

    def finish(g):
        for way in range(2):
            scatter_arrived(way, g, hops(way, g) - 1)
        total = part[g, rows_of(z), :] + partial_in[g, rows_of(z), :]
        total = (total + partial_in[g, ring * span : (ring + 1) * span, :]) * factor
        mask = support[g * span : (g + 1) * span, :].astype(jnp.float32)
        for c in range(2):
            out[0, c, g * span : (g + 1) * span, :] = total[:, c * size : (c + 1) * size] * mask

    pull(0)
    pull(1)
    for slot in range(groups + half):
        if slot < groups:
            collect(slot)
        if slot + 2 < groups:
            pull(slot + 2)
        for t in range(1, half):
            if 0 <= slot - t < groups:
                advance(slot - t, t)
        if 0 <= slot - half < groups:
            finish(slot - half)

    for copy in sent:
        copy.wait_send()


def local(direction, slits, sources, support, focus, slit_focus, obj_rows, obj_cols, weights):
    row_count = lax.axis_size("row")
    ring = lax.axis_size("field") // J
    size = direction.shape[3]
    src_count, plane_count = sources.shape[0], focus.shape[0]
    bands = src_count * plane_count
    span = size // (row_count * GROUPS)
    slab = span * row_count
    total_slits = slits.shape[0] * lax.axis_size("field")
    cols_t, rows_t, rows = kernel_tables(size, row_count, GROUPS)
    smem = pl.BlockSpec(memory_space=pltpu.SMEM)
    vmem = pl.BlockSpec(memory_space=pltpu.VMEM)
    hbm = pl.BlockSpec(memory_space=pl.ANY)
    dma = pltpu.SemaphoreType.DMA
    half = ring // 2
    peers = row_count - 1
    return pl.pallas_call(
        functools.partial(body, (ring, row_count, src_count, plane_count, size, total_slits)),
        out_shape=jax.ShapeDtypeStruct(direction.shape, jnp.float32),
        in_specs=[smem, smem, smem, smem, vmem, vmem, vmem, vmem, hbm, hbm, hbm, hbm],
        out_specs=vmem,
        scratch_shapes=[
            pltpu.VMEM(cols_t.shape, jnp.float32),
            pltpu.VMEM(rows_t.shape, jnp.float32),
            pltpu.VMEM(rows.shape, jnp.float32),
            pltpu.VMEM((bands, M, M), jnp.float32),
            pltpu.VMEM((J, 4 * span, 128), jnp.float32),
            pltpu.VMEM((GROUPS, ring * span, 2 * size), jnp.bfloat16),
            pltpu.VMEM((slab, ring * span), jnp.bfloat16),
            pltpu.VMEM((ring * span, slab), jnp.bfloat16),
            pltpu.VMEM((128, size), jnp.float32),
            pltpu.VMEM((size, 128), jnp.float32),
            pltpu.VMEM((128, size), jnp.float32),
            pltpu.VMEM((bands * 2 * M, 2 * size), jnp.bfloat16),
            pltpu.VMEM((bands * 2 * M, size), jnp.bfloat16),
            pltpu.VMEM((bands, size, 2 * M), jnp.bfloat16),
            pltpu.VMEM((GROUPS, slab, 2 * size), jnp.bfloat16),
            pltpu.VMEM((GROUPS, slab, 2 * size), jnp.bfloat16),
            pltpu.VMEM((bands, 2 * M, 2 * M), jnp.float32),
            pltpu.VMEM((size, bands * 2 * M), jnp.bfloat16),
            pltpu.VMEM((GROUPS, slab, 2 * size), jnp.bfloat16),
            pltpu.VMEM((GROUPS, slab, 2 * size), jnp.bfloat16),
            pltpu.VMEM((GROUPS, ring * span, 2 * size), jnp.float32),
            pltpu.VMEM((GROUPS, (ring + 1) * span, 2 * size), jnp.float32),
            dma((4,)),
            dma((J - 1,)),
            dma((J - 1,)),
            dma((2, GROUPS, half)),
            dma((2, GROUPS, half)),
            dma((peers, GROUPS)),
            dma((peers, GROUPS)),
            dma((peers, GROUPS)),
            dma((peers, GROUPS)),
            dma((2, GROUPS, half)),
            dma((2, GROUPS, half)),
        ],
        compiler_params=pltpu.CompilerParams(
            collective_id=0, has_side_effects=True, vmem_limit_bytes=56 * 1024 * 1024
        ),
    )(
        slits, sources, focus, slit_focus, direction, support, obj_rows, obj_cols,
        weights.reshape(bands, M, M), cols_t, rows_t, rows,
    )


def solution(mesh):
    return jax.shard_map(
        local,
        mesh=mesh,
        in_specs=(
            P("field", None, "row", None),
            P("field"),
            P(),
            P("row", None),
            P(),
            P("field"),
            P(),
            P(),
            P(),
        ),
        out_specs=P("field", None, "row", None),
        check_vma=False,
    )
```

```python
import functools
import math

import jax
import jax.numpy as jnp
import numpy as np
from jax import lax
from jax.experimental import pallas as pl
from jax.experimental.pallas import tpu as pltpu
from jax.sharding import PartitionSpec as P

J = 4
M = 128
SLIT_GRID = 512
SRC_SIDE = 9
SHIFT = 8
PAD = 32
GROUPS = 4
LEVELS = 32000.0
MESH = pl.DeviceIdType.MESH


def kernel_tables(size, blocks, groups):
    freq = np.arange(size)
    span = size // (blocks * groups)
    order = freq.reshape(blocks, groups, span).transpose(1, 0, 2).reshape(-1)

    def kernel(stretch):
        turns = np.mod(stretch * (freq - size // 2)[:, None] * (np.arange(M) - M // 2)[None, :], size)
        angle = (turns.astype(np.float32) * np.float32(-2.0 * math.pi / size)).astype(np.float64)
        scale = 1.0 / math.sqrt(M)
        return np.stack([np.cos(angle) * scale, np.sin(angle) * scale]).astype(np.float32)

    last = np.stack([kernel(1), kernel(2)[:, order]])
    return np.ascontiguousarray(last.transpose(0, 1, 3, 2)), last


def body(sizes, slits, sources, focus, slit_focus, direction_hbm, support_hbm, obj_rows_hbm, obj_cols_hbm, weights_hbm,
         ker_t_hbm, ker_n_hbm, out_hbm,
         direction, support, obj_rows, obj_cols, weights, ker_t, ker_n, info, coeff, mix, mix_t, pick, fac, fac_c, fac_t, fac_p,
         col_t, row_t, col_n, row_n, pupil_out, pupil_in, spec, image, adj_re, adj_im, pulled, returned, part, part_out, part_in, out,
         load_sem, out_sem, info_send, info_recv, ag_send, ag_recv, out_send, out_recv, back_send, back_recv, rs_send, rs_recv):
    ring, row_count, src_count, plane_count, size, total_slits = sizes
    groups = GROUPS
    span = size // (row_count * groups)
    slab = span * row_count
    bands = src_count * plane_count
    half = ring // 2
    me_f, me_r = lax.axis_index("field"), lax.axis_index("row")
    z, j = me_f // J, me_f % J
    y, x = me_r // 2, me_r % 2
    y_count = row_count // 2
    right = (((z + 1) % ring) * J + j, me_r)
    left = (((z + ring - 1) % ring) * J + j, me_r)
    siblings = [(z * J + (j + d) % J, me_r) for d in range(1, J)]
    steps = [(dy, dx) for dy in (2, 1, 3, 0) for dx in (1, 0) if dy < y_count and (dy, dx) != (0, 0)]
    peers = [((y + dy) % y_count) * 2 + (x + dx) % 2 for dy, dx in steps]

    barrier = pltpu.get_barrier_semaphore()
    greeted = [right, left] + siblings + [(me_f, peer) for peer in peers]
    for device in greeted:
        pl.semaphore_signal(barrier, inc=1, device_id=device, device_id_type=MESH)

    loads = [
        pltpu.make_async_copy(src, dst, load_sem.at[i])
        for i, (src, dst) in enumerate(
            [(direction_hbm, direction), (support_hbm, support), (obj_rows_hbm, obj_rows), (obj_cols_hbm, obj_cols),
             (ker_t_hbm, ker_t), (ker_n_hbm, ker_n), (weights_hbm, weights)]
        )
    ]
    for load in loads:
        load.start()

    def rows_of(k, g=0):
        return pl.ds(pl.multiple_of(g * slab + k * span, span), span)

    def group(g):
        return slice(g * slab, (g + 1) * slab)

    for i in range(2):
        position = (2.0 * slits[i].astype(jnp.float32) + 1.0) / SLIT_GRID - 1.0
        info[j, i * span : (i + 1) * span, :] = jnp.full((span, 128), position, jnp.float32)
        info[j, (2 + i) * span : (3 + i) * span, :] = jnp.full((span, 128), slit_focus[i], jnp.float32)
    loads[0].wait()
    for g in range(groups):
        for c in range(2):
            coeff[rows_of(z, g), c * size : (c + 1) * size] = direction[0, c, g * span : (g + 1) * span, :]

    pl.semaphore_wait(barrier, len(greeted))

    def send(src, dst, send_sem, recv_sem, device):
        copy = pltpu.make_async_remote_copy(
            src_ref=src, dst_ref=dst, send_sem=send_sem, recv_sem=recv_sem, device_id=device, device_id_type=MESH
        )
        copy.start()

    def arrived(dst, send_sem, recv_sem, device):
        pltpu.make_async_remote_copy(
            src_ref=dst, dst_ref=dst, send_sem=send_sem, recv_sem=recv_sem, device_id=device, device_id_type=MESH
        ).wait_recv()

    def hops(way, g):
        return half if way == g % 2 else half - 1

    def ring_to(way):
        return right if way == 0 else left

    def gather_slot(way, g, h):
        k = (z + ring - h) % ring if way == 0 else (z + h) % ring
        return coeff.at[rows_of(k, g), :]

    def gather_send(way, g, h):
        slot = gather_slot(way, g, h)
        send(slot, slot, ag_send.at[0], ag_recv.at[way, g, h], ring_to(way))

    def gather_arrived(way, g, h):
        arrived(gather_slot(way, g, h + 1), ag_send.at[0], ag_recv.at[way, g, h], ring_to(way))

    def windows():
        for load in loads[2:4]:
            load.wait()
        middle = SRC_SIDE // 2
        for axis, spectrum in enumerate((obj_rows, obj_cols)):
            shifted = [spectrum[:, PAD - SHIFT * (v - middle) : PAD - SHIFT * (v - middle) + size] for v in range(SRC_SIDE)]
            for q in range(src_count):
                place = sources[q] // SRC_SIDE if axis == 0 else sources[q] % SRC_SIDE
                picked = shifted[0]
                for v in range(1, SRC_SIDE):
                    picked = jnp.where(place == v, shifted[v], picked)
                pick[axis, 8 * q : 8 * q + 2, :] = picked

    def phases():
        own_focus = info[me_r // 2, pl.ds((2 + me_r % 2) * span, 8), :]
        own_focus = jnp.concatenate([own_focus] * (size // 128), axis=1)
        which = lax.broadcasted_iota(jnp.int32, (8, size), 0)
        plane = jnp.full((8, size), focus[0], jnp.float32)
        for p in range(1, plane_count):
            plane = jnp.where(which == p, focus[p], plane)
        freq = lax.broadcasted_iota(jnp.int32, (8, size), 1)
        scaled = (2 * freq - size + 1).astype(jnp.float32) / size
        theta = math.pi * (plane + own_focus) * (scaled * scaled)
        return jnp.cos(theta), jnp.sin(theta)

    def factors(q, turn_cos, turn_sin):
        for axis in range(2):
            first, second = pick[axis, 8 * q : 8 * q + 1, :], pick[axis, 8 * q + 1 : 8 * q + 2, :]
            base = 64 * axis + 8 * q
            fac[base : base + 8, :] = first * turn_cos - second * turn_sin
            fac[base + 32 : base + 40, :] = first * turn_sin + second * turn_cos

    def turn_factors():
        fac_c[...] = fac[...].T
        for g in range(groups):
            for r in range(row_count):
                start = r * groups * span + g * span
                fac_t[g * slab + r * span : g * slab + (r + 1) * span, :] = fac_c[start : start + span, :]
        fac_p[...] = fac_t[...].T

    def mixing():
        edge = row_count * span
        position = jnp.concatenate([info[s, 0 : 2 * span, :] for s in range(J)], axis=0)
        position = jnp.concatenate([position] * (edge // 128), axis=1) if edge > 128 else position
        sub = lax.broadcasted_iota(jnp.int32, (edge, edge), 0)
        lane = lax.broadcasted_iota(jnp.int32, (edge, edge), 1)
        before, now = jnp.ones_like(position), position
        chosen = jnp.where(lane // span == 0, before, jnp.where(lane // span == 1, now, 0.0))
        for order in range(1, ring - 1):
            before, now = now, ((2.0 * order + 1.0) * position * now - order * before) / (order + 1.0)
            chosen = jnp.where(lane // span == order + 1, now, chosen)
        chosen = jnp.where(sub % span == lane % span, chosen, 0.0)
        mix[...] = chosen.astype(jnp.bfloat16)
        mix_t[...] = chosen.T.astype(jnp.bfloat16)

    def index_of(band):
        return (band // plane_count) * 8 + band % plane_count

    def build_lanes(band, carry):
        index = index_of(band)
        cf_re, cf_im = fac[pl.ds(64 + index, 1), :], fac[pl.ds(96 + index, 1), :]
        rf_re, rf_im = fac_p[pl.ds(index, 1), :], fac_p[pl.ds(32 + index, 1), :]
        col_base, row_base = pl.multiple_of(band * M, M), pl.multiple_of(band * 2 * M, 2 * M)
        for m in range(0, M, 16):
            ker_re, ker_im = ker_t[0, 0, m : m + 16, :], ker_t[0, 1, m : m + 16, :]
            col_t[pl.ds(col_base + m, 16), 0:size] = (cf_re * ker_re - cf_im * ker_im).astype(jnp.bfloat16)
            col_t[pl.ds(col_base + m, 16), size : 2 * size] = (cf_re * ker_im + cf_im * ker_re).astype(jnp.bfloat16)
            ker_re, ker_im = ker_t[1, 0, m : m + 16, :], ker_t[1, 1, m : m + 16, :]
            row_t[pl.ds(row_base + m, 16), :] = (rf_re * ker_re - rf_im * ker_im).astype(jnp.bfloat16)
            row_t[pl.ds(row_base + M + m, 16), :] = (rf_re * ker_im + rf_im * ker_re).astype(jnp.bfloat16)
        return carry

    def build_sublanes(axis, held, offset, table):
        def step(i, carry):
            at = pl.ds(pl.multiple_of(i * 32, 32), 32)
            ker_re, ker_im = ker_n[axis, 0, at, :], ker_n[axis, 1, at, :]
            values = held[at, :]
            for band in range(bands):
                index = offset + index_of(band)
                f_re, f_im = values[:, index : index + 1], values[:, 32 + index : 33 + index]
                table[band, at, 0:M] = (f_re * ker_re - f_im * ker_im).astype(jnp.bfloat16)
                table[band, at, M : 2 * M] = (f_re * ker_im + f_im * ker_re).astype(jnp.bfloat16)
            return carry

        return step

    build_col = build_sublanes(0, fac_c, 64, col_n)
    build_row = build_sublanes(1, fac_t, 0, row_n)
    slices = size // 32

    def start_tables():
        for d in range(J - 1):
            arrived(info.at[(j + J - 1 - d) % J], info_send.at[0], info_recv.at[d], siblings[d])
        turn_cos, turn_sin = phases()
        for q in range(src_count):
            factors(q, turn_cos, turn_sin)
        turn_factors()
        mixing()
        for load in loads[4:6]:
            load.wait()

    def own(g):
        for way in range(2):
            gather_send(way, g, 0)

    def relay(g, h):
        for way in range(2):
            if h <= hops(way, g):
                gather_arrived(way, g, h - 1)
                if h < hops(way, g):
                    gather_send(way, g, h)

    def masked(values, g):
        mask = support[g * span : (g + 1) * span, :].astype(jnp.float32)
        mask = jnp.concatenate([mask, mask], axis=1)
        return values * jnp.concatenate([mask] * (values.shape[0] // span), axis=0)

    def pupils(g):
        relay(g, half)
        summed = jnp.dot(mix[...], coeff[group(g), :], preferred_element_type=jnp.float32)
        pupil_out[group(g), :] = masked(summed, g).astype(jnp.bfloat16)
        for d, peer in enumerate(peers):
            send(
                pupil_out.at[rows_of(peer, g), :], pupil_in.at[rows_of(me_r, g), :],
                out_send.at[0], out_recv.at[g], (me_f, peer),
            )
        pupil_in[rows_of(me_r, g), :] = pupil_out[rows_of(me_r, g), :]

    def build(step, first, last, parts, count):
        lax.fori_loop(first * count // parts, last * count // parts, step, 0)

    for g in range(groups):
        own(g)
    for d, device in enumerate(siblings):
        send(info.at[j], info.at[j], info_send.at[0], info_recv.at[d], device)
    windows()
    cols = 0
    for h in range(1, half):
        for g in range(groups):
            relay(g, h)
            if (h, g) == (1, groups - 1):
                start_tables()
                loads[1].wait()
            if h > 1:
                build(build_col, cols, cols + 1, 2 * groups, slices)
                cols += 1
    build(build_lanes, 0, 1, 2, bands)
    for g in range(groups):
        pupils(g)
    build(build_lanes, 1, 2, 2, bands)

    def exchanged(landed, send_sem, recv_sem, g):
        blocks = landed.at[g * slab : g * slab + len(peers) * span, :]
        arrived(blocks, send_sem.at[0], recv_sem.at[g], (me_f, peers[0]))

    def spectra_of(g, band):
        stacked = jnp.concatenate([pupil_in[group(g), 0:size], pupil_in[group(g), size : 2 * size]], axis=0)
        prod = jnp.dot(stacked, col_n[band], preferred_element_type=jnp.float32)
        real = prod[:slab, :M] - prod[slab:, M:]
        imag = prod[:slab, M:] + prod[slab:, :M]
        return jnp.concatenate([real, imag], axis=1).astype(jnp.bfloat16)

    def spectra(g):
        exchanged(pupil_in, out_send, out_recv, g)

        def step(band, carry):
            spec[band, g % 2 * slab : (g % 2 + 1) * slab, :] = spectra_of(g, band)
            return carry

        lax.fori_loop(0, bands, step, 0, unroll=True)

    def images(g):
        def step(band, carry):
            base = pl.multiple_of(band * 2 * M, 2 * M)
            kernel = row_t[pl.ds(base, 2 * M), g * slab : (g + 2) * slab]
            term = jnp.dot(kernel, spec[band], preferred_element_type=jnp.float32)
            image[band] = term if g == 0 else image[band] + term
            return carry

        lax.fori_loop(0, bands, step, 0, unroll=True)

    def adjoints():
        def step(band, carry):
            term = image[band]
            weight = weights[band]
            real = (weight * (term[:M, :M] - term[M:, M:])).astype(jnp.bfloat16)
            imag = (weight * (term[:M, M:] + term[M:, :M])).astype(jnp.bfloat16)
            square = jnp.concatenate(
                [jnp.concatenate([real, imag], axis=1), jnp.concatenate([imag, -real], axis=1)], axis=0
            )
            back = jnp.dot(row_n[band], square, preferred_element_type=jnp.float32).astype(jnp.bfloat16)
            at = pl.ds(pl.multiple_of(band * M, M), M)
            adj_re[:, at] = back[:, :M]
            adj_im[:, at] = back[:, M:]
            return carry

        lax.fori_loop(0, bands, step, 0, unroll=True)

    spectra(0)
    build(build_row, 0, 1, 2, slices)
    spectra(1)
    images(0)
    build(build_row, 1, 2, 2, slices)
    loads[6].wait()
    spectra(2)
    spectra(3)
    images(2)
    adjoints()

    def pull(g):
        rows = slice(g * slab, (g + 1) * slab)
        stacked = jnp.concatenate([adj_re[rows, :], adj_im[rows, :]], axis=0)
        with_re = jnp.dot(stacked, col_t[:, 0:size], preferred_element_type=jnp.float32)
        with_im = jnp.dot(stacked, col_t[:, size : 2 * size], preferred_element_type=jnp.float32)
        pulled[group(g), 0:size] = (with_re[:slab] + with_im[slab:]).astype(jnp.bfloat16)
        pulled[group(g), size : 2 * size] = (with_re[slab:] - with_im[:slab]).astype(jnp.bfloat16)
        for d, peer in enumerate(peers):
            send(
                pulled.at[rows_of(peer, g), :], returned.at[rows_of(me_r, g), :],
                back_send.at[0], back_recv.at[g], (me_f, peer),
            )
        returned[rows_of(me_r, g), :] = pulled[rows_of(me_r, g), :]

    def target(way, g, t):
        away = hops(way, g) - t
        return (z + away) % ring if way == 0 else (z + ring - away) % ring

    def scatter_slot(way, g, t, k):
        if way == 1 and t == hops(way, g) - 1:
            return part_in.at[g, ring * span : (ring + 1) * span, :]
        return part_in.at[g, rows_of(k), :]

    def coded(values):
        top = jnp.max(jnp.abs(values), axis=1, keepdims=True)
        power = jnp.ceil(jnp.log2(jnp.maximum(jnp.broadcast_to(top, (span, 128)), 2.0**-120)))
        scale = jnp.concatenate([jnp.exp2(-power)] * (2 * size // 128), axis=1)
        levels = jnp.round(values * scale * LEVELS)
        return levels.astype(jnp.int32).astype(jnp.int16), power.astype(jnp.int32).astype(jnp.int16)

    def decoded(slot):
        power = slot[:, 2 * size :].astype(jnp.int32).astype(jnp.float32)
        scale = jnp.concatenate([jnp.exp2(power) * (1.0 / LEVELS)] * (2 * size // 128), axis=1)
        return slot[:, 0 : 2 * size].astype(jnp.int32).astype(jnp.float32) * scale

    def scatter_send(way, g, t):
        k = target(way, g, t)
        levels, power = coded(part[rows_of(k, g), :])
        part_out[rows_of(k, g), 0 : 2 * size] = levels
        part_out[rows_of(k, g), 2 * size :] = power
        send(
            part_out.at[rows_of(k, g), :], scatter_slot(way, g, t, k),
            rs_send.at[0], rs_recv.at[way, g, t], ring_to(way),
        )

    def scatter_arrived(way, g, t):
        k = target(way, g, t + 1) if t + 1 < hops(way, g) else z
        slot = scatter_slot(way, g, t, k)
        arrived(slot, rs_send.at[0], rs_recv.at[way, g, t], ring_to(way))
        return k

    def collect(g):
        exchanged(returned, back_send, back_recv, g)
        part[group(g), :] = jnp.dot(mix_t[...], returned[group(g), :], preferred_element_type=jnp.float32)
        for way in range(2):
            scatter_send(way, g, 0)

    def advance(g, t):
        for way in range(2):
            if t < hops(way, g):
                k = scatter_arrived(way, g, t - 1)
                part[rows_of(k, g), :] = part[rows_of(k, g), :] + decoded(part_in.at[g, rows_of(k), :])
                scatter_send(way, g, t)

    factor = 4.0 / (bands * total_slits)
    leaving = []

    def finish(g):
        for way in range(2):
            scatter_arrived(way, g, hops(way, g) - 1)
        total = part[rows_of(z, g), :] + decoded(part_in.at[g, rows_of(z), :])
        total = (total + decoded(part_in.at[g, ring * span : (ring + 1) * span, :])) * factor
        total = masked(total, g)
        for c in range(2):
            out[g, c] = total[:, c * size : (c + 1) * size]
        leave = pltpu.make_async_copy(out.at[g], out_hbm.at[0, :, g * span : (g + 1) * span, :], out_sem.at[g])
        leave.start()
        leaving.append(leave)

    for g in range(groups):
        pull(g)
    for slot in range(groups + half):
        if slot < groups:
            collect(slot)
        for t in range(1, half):
            if 0 <= slot - t < groups:
                advance(slot - t, t)
        if 0 <= slot - half < groups:
            finish(slot - half)

    rounds = (ring - 1) * groups * span
    for moved, count, sem in (
        (info, J - 1, info_send), (coeff, rounds, ag_send), (pupil_out, len(peers) * groups * span, out_send),
        (pulled, len(peers) * groups * span, back_send), (part_out, rounds, rs_send),
    ):
        all_sent = moved.at[0:count]
        pltpu.make_async_remote_copy(
            src_ref=all_sent, dst_ref=all_sent, send_sem=sem.at[0], recv_sem=sem.at[0], device_id=right, device_id_type=MESH
        ).wait_send()
    for leave in leaving:
        leave.wait()


def local(direction, slits, sources, support, focus, slit_focus, obj_rows, obj_cols, weights):
    row_count = lax.axis_size("row")
    ring = lax.axis_size("field") // J
    size = direction.shape[3]
    src_count, plane_count = sources.shape[0], focus.shape[0]
    bands = src_count * plane_count
    span = size // (row_count * GROUPS)
    slab = span * row_count
    total_slits = slits.shape[0] * lax.axis_size("field")
    ker_t, ker_n = kernel_tables(size, row_count, GROUPS)
    weights = weights.reshape(bands, M, M)
    smem = pl.BlockSpec(memory_space=pltpu.SMEM)
    hbm = pl.BlockSpec(memory_space=pl.ANY)
    dma = pltpu.SemaphoreType.DMA
    half = ring // 2
    peers = row_count - 1
    f32, bf16 = jnp.float32, jnp.bfloat16
    return pl.pallas_call(
        functools.partial(body, (ring, row_count, src_count, plane_count, size, total_slits)),
        out_shape=jax.ShapeDtypeStruct(direction.shape, jnp.float32),
        in_specs=[smem] * 4 + [hbm] * 7,
        out_specs=hbm,
        scratch_shapes=[
            pltpu.VMEM(direction.shape, bf16),
            pltpu.VMEM(support.shape, jnp.int32),
            pltpu.VMEM(obj_rows.shape, f32),
            pltpu.VMEM(obj_cols.shape, f32),
            pltpu.VMEM(weights.shape, f32),
            pltpu.VMEM(ker_t.shape, f32),
            pltpu.VMEM(ker_n.shape, f32),
            pltpu.VMEM((J, 4 * span, 128), f32),
            pltpu.VMEM((GROUPS * ring * span, 2 * size), bf16),
            pltpu.VMEM((slab, ring * span), bf16),
            pltpu.VMEM((ring * span, slab), bf16),
            pltpu.VMEM((2, 8 * src_count, size), f32),
            pltpu.VMEM((128, size), f32),
            pltpu.VMEM((size, 128), f32),
            pltpu.VMEM((size, 128), f32),
            pltpu.VMEM((128, size), f32),
            pltpu.VMEM((bands * M, 2 * size), bf16),
            pltpu.VMEM((bands * 2 * M, size), bf16),
            pltpu.VMEM((bands, size, 2 * M), bf16),
            pltpu.VMEM((bands, size, 2 * M), bf16),
            pltpu.VMEM((GROUPS * slab, 2 * size), bf16),
            pltpu.VMEM((GROUPS * slab, 2 * size), bf16),
            pltpu.VMEM((bands, 2 * slab, 2 * M), bf16),
            pltpu.VMEM((bands, 2 * M, 2 * M), f32),
            pltpu.VMEM((size, bands * M), bf16),
            pltpu.VMEM((size, bands * M), bf16),
            pltpu.VMEM((GROUPS * slab, 2 * size), bf16),
            pltpu.VMEM((GROUPS * slab, 2 * size), bf16),
            pltpu.VMEM((GROUPS * ring * span, 2 * size), f32),
            pltpu.VMEM((GROUPS * ring * span, 2 * size + 128), jnp.int16),
            pltpu.VMEM((GROUPS, (ring + 1) * span, 2 * size + 128), jnp.int16),
            pltpu.VMEM((GROUPS, 2, span, size), f32),
            dma((7,)),
            dma((GROUPS,)),
            dma((1,)),
            dma((J - 1,)),
            dma((1,)),
            dma((2, GROUPS, half)),
            dma((1,)),
            dma((GROUPS,)),
            dma((1,)),
            dma((GROUPS,)),
            dma((1,)),
            dma((2, GROUPS, half)),
        ],
        compiler_params=pltpu.CompilerParams(
            collective_id=0, has_side_effects=True, vmem_limit_bytes=56 * 1024 * 1024
        ),
    )(slits, sources, focus, slit_focus, direction, support, obj_rows, obj_cols, weights, ker_t, ker_n)


def solution(mesh):
    return jax.shard_map(
        local,
        mesh=mesh,
        in_specs=(
            P("field", None, "row", None),
            P("field"),
            P(),
            P("row", None),
            P(),
            P("field"),
            P(),
            P(),
            P(),
        ),
        out_specs=P("field", None, "row", None),
        check_vma=False,
    )
```

```python
import functools
import math

import jax
import jax.numpy as jnp
import numpy as np
from jax import lax
from jax.experimental import pallas as pl
from jax.experimental.pallas import tpu as pltpu
from jax.sharding import PartitionSpec as P

J = 4
M = 128
SLIT_GRID = 512
SRC_SIDE = 9
SHIFT = 8
PAD = 32
GROUPS = 4
LEVELS = 32000.0
MESH = pl.DeviceIdType.MESH


def kernel_tables(size, blocks, groups):
    freq = np.arange(size)
    span = size // (blocks * groups)
    order = freq.reshape(blocks, groups, span).transpose(1, 0, 2).reshape(-1)

    def kernel(stretch):
        turns = np.mod(stretch * (freq - size // 2)[:, None] * (np.arange(M) - M // 2)[None, :], size)
        angle = (turns.astype(np.float32) * np.float32(-2.0 * math.pi / size)).astype(np.float64)
        scale = 1.0 / math.sqrt(M)
        return np.stack([np.cos(angle) * scale, np.sin(angle) * scale]).astype(np.float32)

    last = np.stack([kernel(1), kernel(2)[:, order]])
    return np.ascontiguousarray(last.transpose(0, 1, 3, 2)), last


def body(sizes, slits, sources, focus, slit_focus, direction_hbm, support_hbm, obj_rows_hbm, obj_cols_hbm, weights_hbm,
         ker_t_hbm, ker_n_hbm, out_hbm,
         direction, support, obj_rows, obj_cols, weights, ker_t, ker_n, info, coeff, mix, mix_t, pick, fac, fac_c, fac_t, fac_p,
         col_t, row_t, col_n, row_n, pupil_out, pupil_in, spec, image, adj_re, adj_im, pulled, returned, part, part_out, part_in, out,
         load_sem, out_sem, info_send, info_recv, ag_send, ag_recv, out_send, out_recv, back_send, back_recv, rs_send, rs_recv):
    ring, row_count, src_count, plane_count, size = sizes
    groups = GROUPS
    span = size // (row_count * groups)
    slab = span * row_count
    bands = src_count * plane_count
    half = ring // 2
    me_f, me_r = lax.axis_index("field"), lax.axis_index("row")
    z, j = me_f // J, me_f % J
    y, x = me_r // 2, me_r % 2
    y_count = row_count // 2

    def ahead(way, n):
        return (z + n) % ring if way == 0 else (z + ring - n) % ring

    def ring_to(way, n=1):
        return (ahead(way, n) * J + j, me_r)

    right = ring_to(0)
    siblings = [(z * J + (j + d) % J, me_r) for d in range(1, J)]
    steps = [(dy, dx) for dy in (2, 1, 3, 0) for dx in (1, 0) if dy < y_count and (dy, dx) != (0, 0)]
    peers = [((y + dy) % y_count) * 2 + (x + dx) % 2 for dy, dx in steps]

    barrier = pltpu.get_barrier_semaphore()
    greeted = [ring_to(way, n) for way in range(2) for n in (1, 2, 3)] + siblings + [(me_f, peer) for peer in peers]
    for device in greeted:
        pl.semaphore_signal(barrier, inc=1, device_id=device, device_id_type=MESH)

    loads = [
        pltpu.make_async_copy(src, dst, load_sem.at[i])
        for i, (src, dst) in enumerate(
            [(direction_hbm, direction), (support_hbm, support), (obj_rows_hbm, obj_rows), (obj_cols_hbm, obj_cols),
             (ker_t_hbm, ker_t), (ker_n_hbm, ker_n), (weights_hbm, weights)]
        )
    ]
    for load in loads:
        load.start()

    def rows_of(k, g=0):
        return pl.ds(pl.multiple_of(g * slab + k * span, span), span)

    def group(g):
        return slice(g * slab, (g + 1) * slab)

    for i in range(2):
        position = (2.0 * slits[i].astype(jnp.float32) + 1.0) / SLIT_GRID - 1.0
        info[j, i * span : (i + 1) * span, :] = jnp.full((span, 128), position, jnp.float32)
        info[j, (2 + i) * span : (3 + i) * span, :] = jnp.full((span, 128), slit_focus[i], jnp.float32)
    loads[0].wait()
    for g in range(groups):
        for c in range(2):
            coeff[rows_of(z, g), c * size : (c + 1) * size] = direction[0, c, g * span : (g + 1) * span, :]

    pl.semaphore_wait(barrier, len(greeted))

    def send(src, dst, send_sem, recv_sem, device):
        copy = pltpu.make_async_remote_copy(
            src_ref=src, dst_ref=dst, send_sem=send_sem, recv_sem=recv_sem, device_id=device, device_id_type=MESH
        )
        copy.start()

    def arrived(dst, send_sem, recv_sem, device):
        pltpu.make_async_remote_copy(
            src_ref=dst, dst_ref=dst, send_sem=send_sem, recv_sem=recv_sem, device_id=device, device_id_type=MESH
        ).wait_recv()

    def long_way(g):
        return g % 2

    def gather_slot(way, g, distance):
        return coeff.at[rows_of(ahead(1 - way, distance), g), :]

    def gather_send(way, g, distance, n=1):
        slot = gather_slot(way, g, distance)
        send(slot, slot, ag_send.at[0], ag_recv.at[way, g, distance + n - 1], ring_to(way, n))

    def gather_arrived(way, g, distance):
        arrived(gather_slot(way, g, distance), ag_send.at[0], ag_recv.at[way, g, distance - 1], ring_to(way))

    def windows():
        for load in loads[2:4]:
            load.wait()
        middle = SRC_SIDE // 2
        for axis, spectrum in enumerate((obj_rows, obj_cols)):
            shifted = [spectrum[:, PAD - SHIFT * (v - middle) : PAD - SHIFT * (v - middle) + size] for v in range(SRC_SIDE)]
            for q in range(src_count):
                place = sources[q] // SRC_SIDE if axis == 0 else sources[q] % SRC_SIDE
                picked = shifted[0]
                for v in range(1, SRC_SIDE):
                    picked = jnp.where(place == v, shifted[v], picked)
                pick[axis, 8 * q : 8 * q + 2, :] = picked

    def phases():
        own_focus = info[me_r // 2, pl.ds((2 + me_r % 2) * span, 8), :]
        own_focus = jnp.concatenate([own_focus] * (size // 128), axis=1)
        which = lax.broadcasted_iota(jnp.int32, (8, size), 0)
        plane = jnp.full((8, size), focus[0], jnp.float32)
        for p in range(1, plane_count):
            plane = jnp.where(which == p, focus[p], plane)
        freq = lax.broadcasted_iota(jnp.int32, (8, size), 1)
        scaled = (2 * freq - size + 1).astype(jnp.float32) / size
        theta = math.pi * (plane + own_focus) * (scaled * scaled)
        return jnp.cos(theta), jnp.sin(theta)

    def factors(q, turn_cos, turn_sin):
        for axis in range(2):
            first, second = pick[axis, 8 * q : 8 * q + 1, :], pick[axis, 8 * q + 1 : 8 * q + 2, :]
            base = 64 * axis + 8 * q
            fac[base : base + 8, :] = first * turn_cos - second * turn_sin
            fac[base + 32 : base + 40, :] = first * turn_sin + second * turn_cos

    def turn_factors():
        fac_c[...] = fac[...].T
        for g in range(groups):
            for r in range(row_count):
                start = r * groups * span + g * span
                fac_t[g * slab + r * span : g * slab + (r + 1) * span, :] = fac_c[start : start + span, :]
        fac_p[...] = fac_t[...].T

    def mixing():
        edge = row_count * span
        position = jnp.concatenate([info[s, 0 : 2 * span, :] for s in range(J)], axis=0)
        position = jnp.concatenate([position] * (edge // 128), axis=1) if edge > 128 else position
        sub = lax.broadcasted_iota(jnp.int32, (edge, edge), 0)
        lane = lax.broadcasted_iota(jnp.int32, (edge, edge), 1)
        before, now = jnp.ones_like(position), position
        chosen = jnp.where(lane // span == 0, before, jnp.where(lane // span == 1, now, 0.0))
        for order in range(1, ring - 1):
            before, now = now, ((2.0 * order + 1.0) * position * now - order * before) / (order + 1.0)
            chosen = jnp.where(lane // span == order + 1, now, chosen)
        chosen = jnp.where(sub % span == lane % span, chosen, 0.0)
        mix[...] = chosen.astype(jnp.bfloat16)
        mix_t[...] = chosen.T.astype(jnp.bfloat16)

    def index_of(band):
        return (band // plane_count) * 8 + band % plane_count

    def build_lanes(band, carry):
        index = index_of(band)
        cf_re, cf_im = fac[pl.ds(64 + index, 1), :], fac[pl.ds(96 + index, 1), :]
        rf_re, rf_im = fac_p[pl.ds(index, 1), :], fac_p[pl.ds(32 + index, 1), :]
        col_base, row_base = pl.multiple_of(band * M, M), pl.multiple_of(band * 2 * M, 2 * M)
        for m in range(0, M, 16):
            ker_re, ker_im = ker_t[0, 0, m : m + 16, :], ker_t[0, 1, m : m + 16, :]
            col_t[pl.ds(col_base + m, 16), 0:size] = (cf_re * ker_re - cf_im * ker_im).astype(jnp.bfloat16)
            col_t[pl.ds(col_base + m, 16), size : 2 * size] = (cf_re * ker_im + cf_im * ker_re).astype(jnp.bfloat16)
            ker_re, ker_im = ker_t[1, 0, m : m + 16, :], ker_t[1, 1, m : m + 16, :]
            row_t[pl.ds(row_base + m, 16), :] = (rf_re * ker_re - rf_im * ker_im).astype(jnp.bfloat16)
            row_t[pl.ds(row_base + M + m, 16), :] = (rf_re * ker_im + rf_im * ker_re).astype(jnp.bfloat16)
        return carry

    def build_sublanes(axis, held, offset, table):
        def step(i, carry):
            at = pl.ds(pl.multiple_of(i * 32, 32), 32)
            ker_re, ker_im = ker_n[axis, 0, at, :], ker_n[axis, 1, at, :]
            values = held[at, :]
            for band in range(bands):
                index = offset + index_of(band)
                f_re, f_im = values[:, index : index + 1], values[:, 32 + index : 33 + index]
                table[band, at, 0:M] = (f_re * ker_re - f_im * ker_im).astype(jnp.bfloat16)
                table[band, at, M : 2 * M] = (f_re * ker_im + f_im * ker_re).astype(jnp.bfloat16)
            return carry

        return step

    build_col = build_sublanes(0, fac_c, 64, col_n)
    build_row = build_sublanes(1, fac_t, 0, row_n)
    slices = size // 32

    def start_tables():
        turn_cos, turn_sin = phases()
        for q in range(src_count):
            factors(q, turn_cos, turn_sin)
        turn_factors()
        mixing()
        for load in loads[4:6]:
            load.wait()

    def own(g):
        for way in range(2):
            gather_send(way, g, 0)

    def second(g):
        up = long_way(g)
        gather_arrived(up, g, 1)
        gather_send(up, g, 1, 2)
        gather_send(up, g, 1)
        gather_arrived(1 - up, g, 1)
        gather_send(1 - up, g, 1)

    def third(g):
        up = long_way(g)
        gather_arrived(up, g, 3)
        gather_send(up, g, 3)
        gather_arrived(1 - up, g, 2)
        gather_send(1 - up, g, 2)

    def gathered(g):
        up = long_way(g)
        gather_arrived(up, g, 2)
        gather_arrived(up, g, 4)
        gather_arrived(1 - up, g, 3)

    def masked(values, g):
        mask = support[g * span : (g + 1) * span, :].astype(jnp.float32)
        mask = jnp.concatenate([mask, mask], axis=1)
        return values * jnp.concatenate([mask] * (values.shape[0] // span), axis=0)

    def pupils(g):
        gathered(g)
        summed = jnp.dot(mix[...], coeff[group(g), :], preferred_element_type=jnp.float32)
        pupil_out[group(g), :] = masked(summed, g).astype(jnp.bfloat16)
        for d, peer in enumerate(peers):
            send(
                pupil_out.at[rows_of(peer, g), :], pupil_in.at[rows_of(me_r, g), :],
                out_send.at[0], out_recv.at[g], (me_f, peer),
            )
        pupil_in[rows_of(me_r, g), :] = pupil_out[rows_of(me_r, g), :]

    def on_core(core, what):
        pl.when(j % 2 == core)(what)

    def build(step, *parts):
        (start0, stop0), (start1, stop1) = parts
        first = jnp.where(j % 2 == 0, start0, start1)
        lax.fori_loop(first, jnp.where(j % 2 == 0, stop0, stop1), step, 0)

    def build_both(step, start, stop):
        lax.fori_loop(start, stop, step, 0)

    def own_blocks():
        for g in range(groups):
            own(g)

    def second_step():
        for g in range(groups):
            second(g)

    on_core(1, own_blocks)
    for d, device in enumerate(siblings):
        send(info.at[j], info.at[j], info_send.at[0], info_recv.at[d], device)
    windows()
    on_core(1, second_step)
    for d in range(J - 1):
        arrived(info.at[(j + J - 1 - d) % J], info_send.at[0], info_recv.at[d], siblings[d])
    on_core(0, own_blocks)
    start_tables()
    loads[1].wait()
    build(build_col, (0, slices // 2), (0, slices // 2))
    on_core(0, second_step)
    build(build_lanes, (0, bands // 2), (0, 0))
    build(build_row, (0, slices // 4), (0, 0))
    for g in range(groups):
        third(g)
        build_both(build_col, (groups + g) * slices // 8, (groups + g + 1) * slices // 8)
    build(build_row, (slices // 4, slices // 2), (0, 0))
    for g in range(groups):
        pupils(g)
    build(build_lanes, (bands // 2, bands), (0, bands))
    build(build_row, (slices // 2, slices), (0, slices // 4))

    def exchanged(landed, send_sem, recv_sem, g):
        blocks = landed.at[g * slab : g * slab + len(peers) * span, :]
        arrived(blocks, send_sem.at[0], recv_sem.at[g], (me_f, peers[0]))

    def spectra_of(g, band):
        stacked = jnp.concatenate([pupil_in[group(g), 0:size], pupil_in[group(g), size : 2 * size]], axis=0)
        prod = jnp.dot(stacked, col_n[band], preferred_element_type=jnp.float32)
        real = prod[:slab, :M] - prod[slab:, M:]
        imag = prod[:slab, M:] + prod[slab:, :M]
        return jnp.concatenate([real, imag], axis=1).astype(jnp.bfloat16)

    def spectra(g):
        exchanged(pupil_in, out_send, out_recv, g)

        def step(band, carry):
            spec[band, g % 2 * slab : (g % 2 + 1) * slab, :] = spectra_of(g, band)
            return carry

        lax.fori_loop(0, bands, step, 0, unroll=True)

    def images(g):
        def step(band, carry):
            base = pl.multiple_of(band * 2 * M, 2 * M)
            kernel = row_t[pl.ds(base, 2 * M), g * slab : (g + 2) * slab]
            term = jnp.dot(kernel, spec[band], preferred_element_type=jnp.float32)
            image[band] = term if g == 0 else image[band] + term
            return carry

        lax.fori_loop(0, bands, step, 0, unroll=True)

    def adjoints():
        def step(band, carry):
            term = image[band]
            weight = weights[band]
            real = (weight * (term[:M, :M] - term[M:, M:])).astype(jnp.bfloat16)
            imag = (weight * (term[:M, M:] + term[M:, :M])).astype(jnp.bfloat16)
            square = jnp.concatenate(
                [jnp.concatenate([real, imag], axis=1), jnp.concatenate([imag, -real], axis=1)], axis=0
            )
            back = jnp.dot(row_n[band], square, preferred_element_type=jnp.float32).astype(jnp.bfloat16)
            at = pl.ds(pl.multiple_of(band * M, M), M)
            adj_re[:, at] = back[:, :M]
            adj_im[:, at] = back[:, M:]
            return carry

        lax.fori_loop(0, bands, step, 0, unroll=True)

    loads[6].wait()
    spectra(0)
    spectra(1)
    images(0)
    build(build_row, (0, 0), (slices // 4, slices))
    spectra(2)
    spectra(3)
    images(2)
    adjoints()

    def pull(g):
        rows = slice(g * slab, (g + 1) * slab)
        stacked = jnp.concatenate([adj_re[rows, :], adj_im[rows, :]], axis=0)
        with_re = jnp.dot(stacked, col_t[:, 0:size], preferred_element_type=jnp.float32)
        with_im = jnp.dot(stacked, col_t[:, size : 2 * size], preferred_element_type=jnp.float32)
        pulled[group(g), 0:size] = (with_re[:slab] + with_im[slab:]).astype(jnp.bfloat16)
        pulled[group(g), size : 2 * size] = (with_re[slab:] - with_im[:slab]).astype(jnp.bfloat16)
        for d, peer in enumerate(peers):
            send(
                pulled.at[rows_of(peer, g), :], returned.at[rows_of(me_r, g), :],
                back_send.at[0], back_recv.at[g], (me_f, peer),
            )
        returned[rows_of(me_r, g), :] = pulled[rows_of(me_r, g), :]

    def scatter_slot(g, k):
        return part_in.at[g, rows_of(k), :]

    def coded(values):
        top = jnp.max(jnp.abs(values), axis=1, keepdims=True)
        power = jnp.ceil(jnp.log2(jnp.maximum(jnp.broadcast_to(top, (span, 128)), 2.0**-120)))
        scale = jnp.concatenate([jnp.exp2(-power)] * (2 * size // 128), axis=1)
        levels = jnp.round(values * scale * LEVELS)
        return levels.astype(jnp.int32).astype(jnp.int16), power.astype(jnp.int32).astype(jnp.int16)

    def decoded(slot):
        power = slot[:, 2 * size :].astype(jnp.int32).astype(jnp.float32)
        scale = jnp.concatenate([jnp.exp2(power) * (1.0 / LEVELS)] * (2 * size // 128), axis=1)
        return slot[:, 0 : 2 * size].astype(jnp.int32).astype(jnp.float32) * scale

    def scatter_send(g, k, slot, arrival, device):
        levels, power = coded(part[rows_of(k, g), :])
        part_out[rows_of(k, g), 0 : 2 * size] = levels
        part_out[rows_of(k, g), 2 * size :] = power
        send(part_out.at[rows_of(k, g), :], scatter_slot(g, slot), rs_send.at[0], rs_recv.at[g, arrival], device)

    def scatter_arrived(g, slot, arrival):
        arrived(scatter_slot(g, slot), rs_send.at[0], rs_recv.at[g, arrival], right)
        return decoded(scatter_slot(g, slot))

    def collect(g):
        up = long_way(g)
        exchanged(returned, back_send, back_recv, g)
        part[group(g), :] = jnp.dot(mix_t[...], returned[group(g), :], preferred_element_type=jnp.float32)
        scatter_send(g, ahead(up, 4), ahead(up, 4), 0, ring_to(up))
        scatter_send(g, ahead(1 - up, 3), ahead(1 - up, 3), 1, ring_to(1 - up))
        scatter_send(g, ahead(up, 2), ahead(up, 2), 2, ring_to(up))
        scatter_send(g, ahead(1 - up, 1), ring, 3, ring_to(1 - up))

    def combine(g):
        up = long_way(g)
        for way, n, arrival, slot in ((up, 3, 0, ring + 2), (1 - up, 2, 1, ring + 1), (up, 1, 2, None)):
            k = ahead(way, n)
            part[rows_of(k, g), :] = part[rows_of(k, g), :] + scatter_arrived(g, k, arrival)
            scatter_send(g, k, k if slot is None else slot, arrival + 4, ring_to(way, n))

    leaving = []

    def finish(g):
        total = part[rows_of(z, g), :] + scatter_arrived(g, ring, 3)
        total = total + scatter_arrived(g, ring + 2, 4) + scatter_arrived(g, ring + 1, 5) + scatter_arrived(g, z, 6)
        total = masked(total, g)
        for c in range(2):
            out[g, c] = total[:, c * size : (c + 1) * size]
        leave = pltpu.make_async_copy(out.at[g], out_hbm.at[0, :, g * span : (g + 1) * span, :], out_sem.at[g])
        leave.start()
        leaving.append(leave)

    for g in range(groups):
        pull(g)
    for stage in (collect, combine, finish):
        for g in range(groups):
            stage(g)

    rounds = (ring - 1) * groups * span
    for moved, count, sem in (
        (info, J - 1, info_send), (coeff, rounds, ag_send), (pupil_out, len(peers) * groups * span, out_send),
        (pulled, len(peers) * groups * span, back_send), (part_out, rounds, rs_send),
    ):
        all_sent = moved.at[0:count]
        pltpu.make_async_remote_copy(
            src_ref=all_sent, dst_ref=all_sent, send_sem=sem.at[0], recv_sem=sem.at[0], device_id=right, device_id_type=MESH
        ).wait_send()
    for leave in leaving:
        leave.wait()


def local(direction, slits, sources, support, focus, slit_focus, obj_rows, obj_cols, weights):
    row_count = lax.axis_size("row")
    ring = lax.axis_size("field") // J
    size = direction.shape[3]
    src_count, plane_count = sources.shape[0], focus.shape[0]
    bands = src_count * plane_count
    span = size // (row_count * GROUPS)
    slab = span * row_count
    total_slits = slits.shape[0] * lax.axis_size("field")
    ker_t, ker_n = kernel_tables(size, row_count, GROUPS)
    weights = weights.reshape(bands, M, M)
    smem = pl.BlockSpec(memory_space=pltpu.SMEM)
    hbm = pl.BlockSpec(memory_space=pl.ANY)
    dma = pltpu.SemaphoreType.DMA
    half = ring // 2
    peers = row_count - 1
    f32, bf16 = jnp.float32, jnp.bfloat16
    sums = pl.pallas_call(
        functools.partial(body, (ring, row_count, src_count, plane_count, size)),
        out_shape=jax.ShapeDtypeStruct(direction.shape, jnp.float32),
        in_specs=[smem] * 4 + [hbm] * 7,
        out_specs=hbm,
        scratch_shapes=[
            pltpu.VMEM(direction.shape, bf16),
            pltpu.VMEM(support.shape, jnp.int32),
            pltpu.VMEM(obj_rows.shape, f32),
            pltpu.VMEM(obj_cols.shape, f32),
            pltpu.VMEM(weights.shape, f32),
            pltpu.VMEM(ker_t.shape, f32),
            pltpu.VMEM(ker_n.shape, f32),
            pltpu.VMEM((J, 4 * span, 128), f32),
            pltpu.VMEM((GROUPS * ring * span, 2 * size), bf16),
            pltpu.VMEM((slab, ring * span), bf16),
            pltpu.VMEM((ring * span, slab), bf16),
            pltpu.VMEM((2, 8 * src_count, size), f32),
            pltpu.VMEM((128, size), f32),
            pltpu.VMEM((size, 128), f32),
            pltpu.VMEM((size, 128), f32),
            pltpu.VMEM((128, size), f32),
            pltpu.VMEM((bands * M, 2 * size), bf16),
            pltpu.VMEM((bands * 2 * M, size), bf16),
            pltpu.VMEM((bands, size, 2 * M), bf16),
            pltpu.VMEM((bands, size, 2 * M), bf16),
            pltpu.VMEM((GROUPS * slab, 2 * size), bf16),
            pltpu.VMEM((GROUPS * slab, 2 * size), bf16),
            pltpu.VMEM((bands, 2 * slab, 2 * M), bf16),
            pltpu.VMEM((bands, 2 * M, 2 * M), f32),
            pltpu.VMEM((size, bands * M), bf16),
            pltpu.VMEM((size, bands * M), bf16),
            pltpu.VMEM((GROUPS * slab, 2 * size), bf16),
            pltpu.VMEM((GROUPS * slab, 2 * size), bf16),
            pltpu.VMEM((GROUPS * ring * span, 2 * size), f32),
            pltpu.VMEM((GROUPS * ring * span, 2 * size + 128), jnp.int16),
            pltpu.VMEM((GROUPS, (ring + 3) * span, 2 * size + 128), jnp.int16),
            pltpu.VMEM((GROUPS, 2, span, size), f32),
            dma((7,)),
            dma((GROUPS,)),
            dma((1,)),
            dma((J - 1,)),
            dma((1,)),
            dma((2, GROUPS, half)),
            dma((1,)),
            dma((GROUPS,)),
            dma((1,)),
            dma((GROUPS,)),
            dma((1,)),
            dma((GROUPS, ring - 1)),
        ],
        compiler_params=pltpu.CompilerParams(
            collective_id=0, has_side_effects=True, vmem_limit_bytes=56 * 1024 * 1024
        ),
    )(slits, sources, focus, slit_focus, direction, support, obj_rows, obj_cols, weights, ker_t, ker_n)
    return sums * (4.0 / (bands * total_slits))


def solution(mesh):
    return jax.shard_map(
        local,
        mesh=mesh,
        in_specs=(
            P("field", None, "row", None),
            P("field"),
            P(),
            P("row", None),
            P(),
            P("field"),
            P(),
            P(),
            P(),
        ),
        out_specs=P("field", None, "row", None),
        check_vma=False,
    )
```

```python
import functools
import math

import jax
import jax.numpy as jnp
import numpy as np
from jax import lax
from jax.experimental import pallas as pl
from jax.experimental.pallas import tpu as pltpu
from jax.sharding import PartitionSpec as P

J = 4
M = 128
SLIT_GRID = 512
SRC_SIDE = 9
SHIFT = 8
PAD = 32
GROUPS = 4
LEVELS = 32000.0
MESH = pl.DeviceIdType.MESH


def kernel_tables(size, blocks, groups):
    freq = np.arange(size)
    span = size // (blocks * groups)
    order = freq.reshape(blocks, groups, span).transpose(1, 0, 2).reshape(-1)

    def kernel(stretch):
        turns = np.mod(stretch * (freq - size // 2)[:, None] * (np.arange(M) - M // 2)[None, :], size)
        angle = (turns.astype(np.float32) * np.float32(-2.0 * math.pi / size)).astype(np.float64)
        scale = 1.0 / math.sqrt(M)
        return np.stack([np.cos(angle) * scale, np.sin(angle) * scale]).astype(np.float32)

    last = np.stack([kernel(1), kernel(2)[:, order]])
    return np.ascontiguousarray(last.transpose(0, 1, 3, 2)), last


def body(sizes, slits, sources, focus, slit_focus, direction_hbm, support_hbm, obj_rows_hbm, obj_cols_hbm, weights_hbm,
         ker_t_hbm, ker_n_hbm, out_hbm,
         direction, support, obj_rows, obj_cols, weights, ker_t, ker_n, info, coeff, mix, mix_t, raw, raw_t, raw_p, fac,
         col_t, row_t, col_n, row_n, pupil_out, pupil_in, spec, image, adj_re, adj_im, pulled, returned, part, part_out, part_in, out,
         load_sem, out_sem, info_send, info_recv, ag_send, ag_recv, out_send, out_recv, back_send, back_recv, rs_send, rs_recv):
    ring, row_count, src_count, plane_count, size = sizes
    groups = GROUPS
    span = size // (row_count * groups)
    slab = span * row_count
    bands = src_count * plane_count
    half = ring // 2
    me_f, me_r = lax.axis_index("field"), lax.axis_index("row")
    z, j = me_f // J, me_f % J
    y, x = me_r // 2, me_r % 2
    y_count = row_count // 2

    def ahead(way, n):
        return (z + n) % ring if way == 0 else (z + ring - n) % ring

    def ring_to(way, n=1):
        return (ahead(way, n) * J + j, me_r)

    right = ring_to(0)
    siblings = [(z * J + (j + d) % J, me_r) for d in range(1, J)]
    steps = [(dy, dx) for dy in (2, 1, 3, 0) for dx in (1, 0) if dy < y_count and (dy, dx) != (0, 0)]
    peers = [((y + dy) % y_count) * 2 + (x + dx) % 2 for dy, dx in steps]

    barrier = pltpu.get_barrier_semaphore()
    greeted = [ring_to(way, n) for way in range(2) for n in (1, 2, 3)] + siblings + [(me_f, peer) for peer in peers]
    for device in greeted:
        pl.semaphore_signal(barrier, inc=1, device_id=device, device_id_type=MESH)

    loads = [
        pltpu.make_async_copy(src, dst, load_sem.at[i])
        for i, (src, dst) in enumerate(
            [(direction_hbm, direction), (support_hbm, support), (obj_rows_hbm, obj_rows), (obj_cols_hbm, obj_cols),
             (ker_t_hbm, ker_t), (ker_n_hbm, ker_n), (weights_hbm, weights)]
        )
    ]
    for load in loads:
        load.start()

    def rows_of(k, g=0):
        return pl.ds(pl.multiple_of(g * slab + k * span, span), span)

    def group(g):
        return slice(g * slab, (g + 1) * slab)

    for i in range(2):
        position = (2.0 * slits[i].astype(jnp.float32) + 1.0) / SLIT_GRID - 1.0
        info[j, i * span : (i + 1) * span, :] = jnp.full((span, 128), position, jnp.float32)
        info[j, (2 + i) * span : (3 + i) * span, :] = jnp.full((span, 128), slit_focus[i], jnp.float32)
    loads[0].wait()
    for g in range(groups):
        for c in range(2):
            coeff[rows_of(z, g), c * size : (c + 1) * size] = direction[0, c, g * span : (g + 1) * span, :]

    pl.semaphore_wait(barrier, len(greeted))

    def send(src, dst, send_sem, recv_sem, device):
        copy = pltpu.make_async_remote_copy(
            src_ref=src, dst_ref=dst, send_sem=send_sem, recv_sem=recv_sem, device_id=device, device_id_type=MESH
        )
        copy.start()

    def arrived(dst, send_sem, recv_sem, device):
        pltpu.make_async_remote_copy(
            src_ref=dst, dst_ref=dst, send_sem=send_sem, recv_sem=recv_sem, device_id=device, device_id_type=MESH
        ).wait_recv()

    def long_way(g):
        return g % 2

    def gather_slot(way, g, distance):
        return coeff.at[rows_of(ahead(1 - way, distance), g), :]

    def gather_send(way, g, distance, n=1):
        slot = gather_slot(way, g, distance)
        send(slot, slot, ag_send.at[0], ag_recv.at[way, g, distance + n - 1], ring_to(way, n))

    def gather_arrived(way, g, distance):
        arrived(gather_slot(way, g, distance), ag_send.at[0], ag_recv.at[way, g, distance - 1], ring_to(way))

    def windows():
        for load in loads[2:4]:
            load.wait()
        middle = SRC_SIDE // 2
        for axis, spectrum in enumerate((obj_rows, obj_cols)):
            shifted = [spectrum[:, PAD - SHIFT * (v - middle) : PAD - SHIFT * (v - middle) + size] for v in range(SRC_SIDE)]
            for q in range(src_count):
                place = sources[q] // SRC_SIDE if axis == 0 else sources[q] % SRC_SIDE
                picked = shifted[0]
                for v in range(1, SRC_SIDE):
                    picked = jnp.where(place == v, shifted[v], picked)
                raw[16 + 32 * axis + 8 * q : 18 + 32 * axis + 8 * q, :] = picked

    def phases():
        own_focus = info[me_r // 2, pl.ds((2 + me_r % 2) * span, 8), :]
        own_focus = jnp.concatenate([own_focus] * (size // 128), axis=1)
        which = lax.broadcasted_iota(jnp.int32, (8, size), 0)
        plane = jnp.full((8, size), focus[0], jnp.float32)
        for p in range(1, plane_count):
            plane = jnp.where(which == p, focus[p], plane)
        freq = lax.broadcasted_iota(jnp.int32, (8, size), 1)
        scaled = (2 * freq - size + 1).astype(jnp.float32) / size
        theta = math.pi * (plane + own_focus) * (scaled * scaled)
        raw[0:8, :] = jnp.cos(theta)
        raw[8:16, :] = jnp.sin(theta)

    def factors(axis, source):
        turn_cos, turn_sin = source[0:8, :], source[8:16, :]
        for q in range(src_count):
            start = 16 + 32 * axis + 8 * q
            first, second = source[start : start + 1, :], source[start + 1 : start + 2, :]
            base = 64 * axis + 8 * q
            fac[base : base + 8, :] = first * turn_cos - second * turn_sin
            fac[base + 32 : base + 40, :] = first * turn_sin + second * turn_cos

    def turn_factors():
        raw_t[...] = raw[...].T
        for g in range(groups):
            for r in range(row_count):
                start = r * groups * span + g * span
                raw_p[g * slab + r * span : g * slab + (r + 1) * span, :] = raw_t[start : start + span, :]
        factors(0, raw_p[...].T)
        factors(1, raw[...])

    def mixing():
        edge = row_count * span
        position = jnp.concatenate([info[s, 0 : 2 * span, :] for s in range(J)], axis=0)
        position = jnp.concatenate([position] * (edge // 128), axis=1) if edge > 128 else position
        sub = lax.broadcasted_iota(jnp.int32, (edge, edge), 0)
        lane = lax.broadcasted_iota(jnp.int32, (edge, edge), 1)
        before, now = jnp.ones_like(position), position
        chosen = jnp.where(lane // span == 0, before, jnp.where(lane // span == 1, now, 0.0))
        for order in range(1, ring - 1):
            before, now = now, ((2.0 * order + 1.0) * position * now - order * before) / (order + 1.0)
            chosen = jnp.where(lane // span == order + 1, now, chosen)
        chosen = jnp.where(sub % span == lane % span, chosen, 0.0)
        mix[...] = chosen.astype(jnp.bfloat16)
        mix_t[...] = chosen.T.astype(jnp.bfloat16)

    def index_of(band):
        return (band // plane_count) * 8 + band % plane_count

    def build_lanes(band, carry):
        index = index_of(band)
        cf_re, cf_im = fac[pl.ds(64 + index, 1), :], fac[pl.ds(96 + index, 1), :]
        rf_re, rf_im = fac[pl.ds(index, 1), :], fac[pl.ds(32 + index, 1), :]
        col_base, row_base = pl.multiple_of(band * M, M), pl.multiple_of(band * 2 * M, 2 * M)
        for m in range(0, M, 16):
            ker_re, ker_im = ker_t[0, 0, m : m + 16, :], ker_t[0, 1, m : m + 16, :]
            col_t[pl.ds(col_base + m, 16), 0:size] = (cf_re * ker_re - cf_im * ker_im).astype(jnp.bfloat16)
            col_t[pl.ds(col_base + m, 16), size : 2 * size] = (cf_re * ker_im + cf_im * ker_re).astype(jnp.bfloat16)
            ker_re, ker_im = ker_t[1, 0, m : m + 16, :], ker_t[1, 1, m : m + 16, :]
            row_t[pl.ds(row_base + m, 16), :] = (rf_re * ker_re - rf_im * ker_im).astype(jnp.bfloat16)
            row_t[pl.ds(row_base + M + m, 16), :] = (rf_re * ker_im + rf_im * ker_re).astype(jnp.bfloat16)
        return carry

    def build_sublanes(axis, held, table):
        def step(i, carry):
            at = pl.ds(pl.multiple_of(i * 32, 32), 32)
            ker_re, ker_im = ker_n[1 - axis, 0, at, :], ker_n[1 - axis, 1, at, :]
            values = held[at, :]
            turned = []
            for p in range(plane_count):
                turn_cos, turn_sin = values[:, p : p + 1], values[:, 8 + p : 9 + p]
                turned.append((turn_cos * ker_re - turn_sin * ker_im, turn_cos * ker_im + turn_sin * ker_re))
            for q in range(src_count):
                start = 16 + 32 * axis + 8 * q
                first = jnp.broadcast_to(values[:, start : start + 1], (32, M))
                second = jnp.broadcast_to(values[:, start + 1 : start + 2], (32, M))
                for p, (real, imag) in enumerate(turned):
                    band = q * plane_count + p
                    table[band, at, 0:M] = (first * real - second * imag).astype(jnp.bfloat16)
                    table[band, at, M : 2 * M] = (first * imag + second * real).astype(jnp.bfloat16)
            return carry

        return step

    build_col = build_sublanes(1, raw_t, col_n)
    build_row = build_sublanes(0, raw_p, row_n)
    slices = size // 32

    def start_tables():
        phases()
        turn_factors()
        mixing()
        for load in loads[4:6]:
            load.wait()

    def own(g):
        for way in range(2):
            gather_send(way, g, 0)

    def second(g):
        up = long_way(g)
        gather_arrived(up, g, 1)
        gather_send(up, g, 1, 2)
        gather_send(up, g, 1)
        gather_arrived(1 - up, g, 1)
        gather_send(1 - up, g, 1)

    def third(g):
        up = long_way(g)
        gather_arrived(up, g, 3)
        gather_send(up, g, 3)
        gather_arrived(1 - up, g, 2)
        gather_send(1 - up, g, 2)

    def gathered(g):
        up = long_way(g)
        gather_arrived(up, g, 2)
        gather_arrived(up, g, 4)
        gather_arrived(1 - up, g, 3)

    def masked(values, g):
        mask = support[g * span : (g + 1) * span, :].astype(jnp.float32)
        mask = jnp.concatenate([mask, mask], axis=1)
        return values * jnp.concatenate([mask] * (values.shape[0] // span), axis=0)

    def pupils(g):
        gathered(g)
        summed = jnp.dot(mix[...], coeff[group(g), :], preferred_element_type=jnp.float32)
        pupil_out[group(g), :] = masked(summed, g).astype(jnp.bfloat16)
        for d, peer in enumerate(peers):
            send(
                pupil_out.at[rows_of(peer, g), :], pupil_in.at[rows_of(me_r, g), :],
                out_send.at[0], out_recv.at[g], (me_f, peer),
            )
        pupil_in[rows_of(me_r, g), :] = pupil_out[rows_of(me_r, g), :]

    def on_core(core, what):
        pl.when(j % 2 == core)(what)

    def build(step, *parts):
        (start0, stop0), (start1, stop1) = parts
        first = jnp.where(j % 2 == 0, start0, start1)
        lax.fori_loop(first, jnp.where(j % 2 == 0, stop0, stop1), step, 0)

    def own_blocks():
        for g in range(groups):
            own(g)

    def second_step():
        for g in range(groups):
            second(g)

    on_core(1, own_blocks)
    for d, device in enumerate(siblings):
        send(info.at[j], info.at[j], info_send.at[0], info_recv.at[d], device)
    windows()
    on_core(0, own_blocks)
    on_core(1, second_step)
    for d in range(J - 1):
        arrived(info.at[(j + J - 1 - d) % J], info_send.at[0], info_recv.at[d], siblings[d])
    start_tables()
    loads[1].wait()
    on_core(0, second_step)
    build(build_lanes, (0, bands // 2), (0, 0))
    build(build_row, (0, slices // 2), (0, 0))
    build(build_col, (0, slices // 2), (0, slices // 2))
    for g in range(groups):
        third(g)
        build(build_row, (0, 0), (g * slices // 8, (g + 1) * slices // 8))
    build(build_col, (slices // 2, slices), (slices // 2, 5 * slices // 8))
    for g in range(groups):
        pupils(g)
    build(build_col, (0, 0), (5 * slices // 8, slices))
    build(build_lanes, (bands // 2, bands), (0, bands))
    build(build_row, (slices // 2, slices), (0, 0))

    def exchanged(landed, send_sem, recv_sem, g):
        blocks = landed.at[g * slab : g * slab + len(peers) * span, :]
        arrived(blocks, send_sem.at[0], recv_sem.at[g], (me_f, peers[0]))

    def spectra_of(g, band):
        stacked = jnp.concatenate([pupil_in[group(g), 0:size], pupil_in[group(g), size : 2 * size]], axis=0)
        prod = jnp.dot(stacked, col_n[band], preferred_element_type=jnp.float32)
        real = prod[:slab, :M] - prod[slab:, M:]
        imag = prod[:slab, M:] + prod[slab:, :M]
        return jnp.concatenate([real, imag], axis=1).astype(jnp.bfloat16)

    def spectra(g):
        exchanged(pupil_in, out_send, out_recv, g)

        def step(band, carry):
            spec[band, g % 2 * slab : (g % 2 + 1) * slab, :] = spectra_of(g, band)
            return carry

        lax.fori_loop(0, bands, step, 0, unroll=True)

    def images(g):
        def step(band, carry):
            base = pl.multiple_of(band * 2 * M, 2 * M)
            kernel = row_t[pl.ds(base, 2 * M), g * slab : (g + 2) * slab]
            term = jnp.dot(kernel, spec[band], preferred_element_type=jnp.float32)
            image[band] = term if g == 0 else image[band] + term
            return carry

        lax.fori_loop(0, bands, step, 0, unroll=True)

    def adjoints():
        def step(band, carry):
            term = image[band]
            weight = weights[band]
            real = (weight * (term[:M, :M] - term[M:, M:])).astype(jnp.bfloat16)
            imag = (weight * (term[:M, M:] + term[M:, :M])).astype(jnp.bfloat16)
            square = jnp.concatenate(
                [jnp.concatenate([real, imag], axis=1), jnp.concatenate([imag, -real], axis=1)], axis=0
            )
            back = jnp.dot(row_n[band], square, preferred_element_type=jnp.float32).astype(jnp.bfloat16)
            at = pl.ds(pl.multiple_of(band * M, M), M)
            adj_re[:, at] = back[:, :M]
            adj_im[:, at] = back[:, M:]
            return carry

        lax.fori_loop(0, bands, step, 0, unroll=True)

    loads[6].wait()
    spectra(0)
    spectra(1)
    images(0)
    build(build_row, (0, 0), (slices // 2, slices))
    spectra(2)
    spectra(3)
    images(2)
    adjoints()

    def pull(g):
        rows = slice(g * slab, (g + 1) * slab)
        stacked = jnp.concatenate([adj_re[rows, :], adj_im[rows, :]], axis=0)
        with_re = jnp.dot(stacked, col_t[:, 0:size], preferred_element_type=jnp.float32)
        with_im = jnp.dot(stacked, col_t[:, size : 2 * size], preferred_element_type=jnp.float32)
        pulled[group(g), 0:size] = (with_re[:slab] + with_im[slab:]).astype(jnp.bfloat16)
        pulled[group(g), size : 2 * size] = (with_re[slab:] - with_im[:slab]).astype(jnp.bfloat16)
        for d, peer in enumerate(peers):
            send(
                pulled.at[rows_of(peer, g), :], returned.at[rows_of(me_r, g), :],
                back_send.at[0], back_recv.at[g], (me_f, peer),
            )
        returned[rows_of(me_r, g), :] = pulled[rows_of(me_r, g), :]

    def scatter_slot(g, k):
        return part_in.at[g, rows_of(k), :]

    def coded(values):
        top = jnp.max(jnp.abs(values), axis=1, keepdims=True)
        power = jnp.ceil(jnp.log2(jnp.maximum(jnp.broadcast_to(top, (span, 128)), 2.0**-120)))
        scale = jnp.concatenate([jnp.exp2(-power)] * (2 * size // 128), axis=1)
        levels = jnp.round(values * scale * LEVELS)
        return levels.astype(jnp.int32).astype(jnp.int16), power.astype(jnp.int32).astype(jnp.int16)

    def decoded(slot):
        power = slot[:, 2 * size :].astype(jnp.int32).astype(jnp.float32)
        scale = jnp.concatenate([jnp.exp2(power) * (1.0 / LEVELS)] * (2 * size // 128), axis=1)
        return slot[:, 0 : 2 * size].astype(jnp.int32).astype(jnp.float32) * scale

    def scatter_send(g, k, slot, arrival, device):
        levels, power = coded(part[rows_of(k, g), :])
        part_out[rows_of(k, g), 0 : 2 * size] = levels
        part_out[rows_of(k, g), 2 * size :] = power
        send(part_out.at[rows_of(k, g), :], scatter_slot(g, slot), rs_send.at[0], rs_recv.at[g, arrival], device)

    def scatter_arrived(g, slot, arrival):
        arrived(scatter_slot(g, slot), rs_send.at[0], rs_recv.at[g, arrival], right)
        return decoded(scatter_slot(g, slot))

    def take_in(g, k, slot, arrival):
        part[rows_of(k, g), :] = part[rows_of(k, g), :] + scatter_arrived(g, slot, arrival)

    def collect(g):
        up = long_way(g)
        exchanged(returned, back_send, back_recv, g)
        part[group(g), :] = jnp.dot(mix_t[...], returned[group(g), :], preferred_element_type=jnp.float32)
        scatter_send(g, ahead(up, 4), ahead(up, 4), 0, ring_to(up))
        scatter_send(g, ahead(1 - up, 3), ahead(1 - up, 3), 1, ring_to(1 - up))

        def more():
            scatter_send(g, ahead(up, 2), ahead(up, 2), 2, ring_to(up))
            if g >= groups // 2:
                scatter_send(g, ahead(1 - up, 1), ring, 3, ring_to(1 - up))

        on_core(0, more)

    def pass_on(g, way, n, arrival, slot, next_arrival):
        k = ahead(way, n)
        take_in(g, k, k, arrival)
        scatter_send(g, k, k if slot is None else slot, next_arrival, ring_to(way))

    def combine_two(g):
        up = long_way(g)
        for way, n, arrival, slot in ((up, 3, 0, ring + 2), (1 - up, 2, 1, ring + 1), (up, 1, 2, None)):
            k = ahead(way, n)
            take_in(g, k, k, arrival)
            scatter_send(g, k, k if slot is None else slot, arrival + 4, ring_to(way, n))

    def combine_three(g):
        up = long_way(g)
        far, near = ahead(up, 3), ahead(1 - up, 2)
        take_in(g, far, far, 0)
        scatter_send(g, far, ring + 2, 4, ring_to(up, 2))
        take_in(g, near, near, 1)
        scatter_send(g, near, near, 5, ring_to(1 - up))

    def deliver_three(g):
        up = long_way(g)
        first, other = ahead(up, 1), ahead(1 - up, 1)
        take_in(g, other, other, 5)
        scatter_send(g, other, ring, 3, ring_to(1 - up))
        take_in(g, first, first, 2)
        take_in(g, first, ring + 2, 4)
        scatter_send(g, first, first, 6, ring_to(up))

    def leave(g):
        return pltpu.make_async_copy(out.at[g], out_hbm.at[0, :, g * span : (g + 1) * span, :], out_sem.at[g])

    def finish(g, *arrivals):
        total = part[rows_of(z, g), :] + scatter_arrived(g, z, 6)
        for slot, arrival in arrivals:
            total = total + scatter_arrived(g, slot, arrival)
        total = masked(total, g)
        for c in range(2):
            out[g, c] = total[:, c * size : (c + 1) * size]
        leave(g).start()

    def with_jumps():
        for g in range(groups):
            (combine_three if g < groups // 2 else combine_two)(g)
        for g in range(groups // 2):
            deliver_three(g)
        for g in range(groups):
            finish(g, *[(ring, 3), (ring + 2, 4), (ring + 1, 5)][: 1 if g < groups // 2 else 3])

    def place_to_place():
        for g in range(groups):
            pass_on(g, long_way(g), 3, 0, None, 2)
            pass_on(g, 1 - long_way(g), 2, 1, None, 4)
        for g in range(groups):
            pass_on(g, long_way(g), 2, 2, None, 5)
            pass_on(g, 1 - long_way(g), 1, 4, ring, 3)
        for g in range(groups):
            pass_on(g, long_way(g), 1, 5, None, 6)
        for g in range(groups):
            finish(g, (ring, 3))

    for g in range(groups):
        pull(g)
    for g in range(groups):
        collect(g)
    on_core(0, with_jumps)
    on_core(1, place_to_place)

    rounds = (ring - 1) * groups * span
    for moved, count, sem in (
        (info, J - 1, info_send), (coeff, rounds, ag_send), (pupil_out, len(peers) * groups * span, out_send),
        (pulled, len(peers) * groups * span, back_send), (part_out, rounds, rs_send),
    ):
        all_sent = moved.at[0:count]
        pltpu.make_async_remote_copy(
            src_ref=all_sent, dst_ref=all_sent, send_sem=sem.at[0], recv_sem=sem.at[0], device_id=right, device_id_type=MESH
        ).wait_send()
    for g in range(groups):
        leave(g).wait()


def local(direction, slits, sources, support, focus, slit_focus, obj_rows, obj_cols, weights):
    row_count = lax.axis_size("row")
    ring = lax.axis_size("field") // J
    size = direction.shape[3]
    src_count, plane_count = sources.shape[0], focus.shape[0]
    bands = src_count * plane_count
    span = size // (row_count * GROUPS)
    slab = span * row_count
    total_slits = slits.shape[0] * lax.axis_size("field")
    ker_t, ker_n = kernel_tables(size, row_count, GROUPS)
    weights = weights.reshape(bands, M, M)
    smem = pl.BlockSpec(memory_space=pltpu.SMEM)
    hbm = pl.BlockSpec(memory_space=pl.ANY)
    dma = pltpu.SemaphoreType.DMA
    half = ring // 2
    peers = row_count - 1
    f32, bf16 = jnp.float32, jnp.bfloat16
    sums = pl.pallas_call(
        functools.partial(body, (ring, row_count, src_count, plane_count, size)),
        out_shape=jax.ShapeDtypeStruct(direction.shape, jnp.float32),
        in_specs=[smem] * 4 + [hbm] * 7,
        out_specs=hbm,
        scratch_shapes=[
            pltpu.VMEM(direction.shape, bf16),
            pltpu.VMEM(support.shape, jnp.int32),
            pltpu.VMEM(obj_rows.shape, f32),
            pltpu.VMEM(obj_cols.shape, f32),
            pltpu.VMEM(weights.shape, f32),
            pltpu.VMEM(ker_t.shape, f32),
            pltpu.VMEM(ker_n.shape, f32),
            pltpu.VMEM((J, 4 * span, 128), f32),
            pltpu.VMEM((GROUPS * ring * span, 2 * size), bf16),
            pltpu.VMEM((slab, ring * span), bf16),
            pltpu.VMEM((ring * span, slab), bf16),
            pltpu.VMEM((128, size), f32),
            pltpu.VMEM((size, 128), f32),
            pltpu.VMEM((size, 128), f32),
            pltpu.VMEM((128, size), f32),
            pltpu.VMEM((bands * M, 2 * size), bf16),
            pltpu.VMEM((bands * 2 * M, size), bf16),
            pltpu.VMEM((bands, size, 2 * M), bf16),
            pltpu.VMEM((bands, size, 2 * M), bf16),
            pltpu.VMEM((GROUPS * slab, 2 * size), bf16),
            pltpu.VMEM((GROUPS * slab, 2 * size), bf16),
            pltpu.VMEM((bands, 2 * slab, 2 * M), bf16),
            pltpu.VMEM((bands, 2 * M, 2 * M), f32),
            pltpu.VMEM((size, bands * M), bf16),
            pltpu.VMEM((size, bands * M), bf16),
            pltpu.VMEM((GROUPS * slab, 2 * size), bf16),
            pltpu.VMEM((GROUPS * slab, 2 * size), bf16),
            pltpu.VMEM((GROUPS * ring * span, 2 * size), f32),
            pltpu.VMEM((GROUPS * ring * span, 2 * size + 128), jnp.int16),
            pltpu.VMEM((GROUPS, (ring + 3) * span, 2 * size + 128), jnp.int16),
            pltpu.VMEM((GROUPS, 2, span, size), f32),
            dma((7,)),
            dma((GROUPS,)),
            dma((1,)),
            dma((J - 1,)),
            dma((1,)),
            dma((2, GROUPS, half)),
            dma((1,)),
            dma((GROUPS,)),
            dma((1,)),
            dma((GROUPS,)),
            dma((1,)),
            dma((GROUPS, ring - 1)),
        ],
        compiler_params=pltpu.CompilerParams(
            collective_id=0, has_side_effects=True, vmem_limit_bytes=56 * 1024 * 1024
        ),
    )(slits, sources, focus, slit_focus, direction, support, obj_rows, obj_cols, weights, ker_t, ker_n)
    return sums * (4.0 / (bands * total_slits))


def solution(mesh):
    return jax.shard_map(
        local,
        mesh=mesh,
        in_specs=(
            P("field", None, "row", None),
            P("field"),
            P(),
            P("row", None),
            P(),
            P("field"),
            P(),
            P(),
            P(),
        ),
        out_specs=P("field", None, "row", None),
        check_vma=False,
    )
```

```python
import functools
import math

import jax
import jax.numpy as jnp
import numpy as np
from jax import lax
from jax.experimental import pallas as pl
from jax.experimental.pallas import tpu as pltpu
from jax.sharding import PartitionSpec as P

J = 4
M = 128
SLIT_GRID = 512
SRC_SIDE = 9
SHIFT = 8
PAD = 32
GROUPS = 4
LEVELS = 32000.0
MESH = pl.DeviceIdType.MESH


def kernel_tables(size, blocks, groups):
    freq = np.arange(size)
    span = size // (blocks * groups)
    order = freq.reshape(blocks, groups, span).transpose(1, 0, 2).reshape(-1)

    def kernel(stretch):
        turns = np.mod(stretch * (freq - size // 2)[:, None] * (np.arange(M) - M // 2)[None, :], size)
        angle = (turns.astype(np.float32) * np.float32(-2.0 * math.pi / size)).astype(np.float64)
        scale = 1.0 / math.sqrt(M)
        return np.stack([np.cos(angle) * scale, np.sin(angle) * scale]).astype(np.float32)

    last = np.stack([kernel(1), kernel(2)[:, order]])
    return np.ascontiguousarray(last.transpose(0, 1, 3, 2)), last


def body(sizes, slits, sources, focus, slit_focus, direction_hbm, support_hbm, obj_rows_hbm, obj_cols_hbm, weights_hbm,
         ker_t_hbm, ker_n_hbm, out_hbm,
         direction, support, obj_rows, obj_cols, weights, ker_t, ker_n, info, coeff, mix, mix_t, raw, raw_t, raw_p, fac,
         col_t, row_t, col_n, row_n, pupil_out, pupil_in, spec, image, adj_re, adj_im, pulled, returned, part, part_out, part_in, out,
         load_sem, out_sem, info_send, info_recv, ag_send, ag_recv, out_send, out_recv, back_send, back_recv, rs_send, rs_recv):
    ring, row_count, src_count, plane_count, size = sizes
    groups = GROUPS
    span = size // (row_count * groups)
    slab = span * row_count
    bands = src_count * plane_count
    half = ring // 2
    me_f, me_r = lax.axis_index("field"), lax.axis_index("row")
    z, j = me_f // J, me_f % J
    y, x = me_r // 2, me_r % 2
    y_count = row_count // 2

    def ahead(way, n):
        return (z + n) % ring if way == 0 else (z + ring - n) % ring

    def ring_to(way, n=1):
        return (ahead(way, n) * J + j, me_r)

    right = ring_to(0)
    siblings = [(z * J + (j + d) % J, me_r) for d in range(1, J)]
    steps = [(2, 1), (1, 0), (3, 1), (2, 0), (1, 1), (3, 0), (0, 1)]
    steps = [(dy, dx) for dy, dx in steps if dy < y_count]
    peers = [((y + dy) % y_count) * 2 + (x + dx) % 2 for dy, dx in steps]

    barrier = pltpu.get_barrier_semaphore()
    greeted = [ring_to(way, n) for way in range(2) for n in (1, 2, 3)] + siblings + [(me_f, peer) for peer in peers]
    for device in greeted:
        pl.semaphore_signal(barrier, inc=1, device_id=device, device_id_type=MESH)

    loads = [
        pltpu.make_async_copy(src, dst, load_sem.at[i])
        for i, (src, dst) in enumerate(
            [(direction_hbm, direction), (support_hbm, support), (obj_rows_hbm, obj_rows), (obj_cols_hbm, obj_cols),
             (ker_t_hbm, ker_t), (ker_n_hbm, ker_n), (weights_hbm, weights)]
        )
    ]
    for load in loads:
        load.start()

    def rows_of(k, g=0):
        return pl.ds(pl.multiple_of(g * slab + k * span, span), span)

    def group(g):
        return slice(g * slab, (g + 1) * slab)

    for i in range(2):
        position = (2.0 * slits[i].astype(jnp.float32) + 1.0) / SLIT_GRID - 1.0
        info[j, i * span : (i + 1) * span, :] = jnp.full((span, 128), position, jnp.float32)
        info[j, (2 + i) * span : (3 + i) * span, :] = jnp.full((span, 128), slit_focus[i], jnp.float32)
    loads[0].wait()
    for g in range(groups):
        for c in range(2):
            coeff[rows_of(z, g), c * size : (c + 1) * size] = direction[0, c, g * span : (g + 1) * span, :]

    pl.semaphore_wait(barrier, len(greeted))

    def send(src, dst, send_sem, recv_sem, device):
        copy = pltpu.make_async_remote_copy(
            src_ref=src, dst_ref=dst, send_sem=send_sem, recv_sem=recv_sem, device_id=device, device_id_type=MESH
        )
        copy.start()

    def arrived(dst, send_sem, recv_sem, device):
        pltpu.make_async_remote_copy(
            src_ref=dst, dst_ref=dst, send_sem=send_sem, recv_sem=recv_sem, device_id=device, device_id_type=MESH
        ).wait_recv()

    def long_way(g):
        return g % 2

    def gather_slot(way, g, distance):
        return coeff.at[rows_of(ahead(1 - way, distance), g), :]

    def gather_send(way, g, distance, n=1):
        slot = gather_slot(way, g, distance)
        send(slot, slot, ag_send.at[0], ag_recv.at[way, g, distance + n - 1], ring_to(way, n))

    def gather_arrived(way, g, distance):
        arrived(gather_slot(way, g, distance), ag_send.at[0], ag_recv.at[way, g, distance - 1], ring_to(way))

    def windows():
        for load in loads[2:4]:
            load.wait()
        middle = SRC_SIDE // 2
        for axis, spectrum in enumerate((obj_rows, obj_cols)):
            shifted = [spectrum[:, PAD - SHIFT * (v - middle) : PAD - SHIFT * (v - middle) + size] for v in range(SRC_SIDE)]
            for q in range(src_count):
                place = sources[q] // SRC_SIDE if axis == 0 else sources[q] % SRC_SIDE
                picked = shifted[0]
                for v in range(1, SRC_SIDE):
                    picked = jnp.where(place == v, shifted[v], picked)
                raw[16 + 32 * axis + 8 * q : 18 + 32 * axis + 8 * q, :] = picked

    def phases():
        own_focus = info[me_r // 2, pl.ds((2 + me_r % 2) * span, 8), :]
        own_focus = jnp.concatenate([own_focus] * (size // 128), axis=1)
        which = lax.broadcasted_iota(jnp.int32, (8, size), 0)
        plane = jnp.full((8, size), focus[0], jnp.float32)
        for p in range(1, plane_count):
            plane = jnp.where(which == p, focus[p], plane)
        freq = lax.broadcasted_iota(jnp.int32, (8, size), 1)
        scaled = (2 * freq - size + 1).astype(jnp.float32) / size
        theta = math.pi * (plane + own_focus) * (scaled * scaled)
        raw[0:8, :] = jnp.cos(theta)
        raw[8:16, :] = jnp.sin(theta)

    def factors(axis, source):
        turn_cos, turn_sin = source[0:8, :], source[8:16, :]
        for q in range(src_count):
            start = 16 + 32 * axis + 8 * q
            first, second = source[start : start + 1, :], source[start + 1 : start + 2, :]
            base = 64 * axis + 8 * q
            fac[base : base + 8, :] = first * turn_cos - second * turn_sin
            fac[base + 32 : base + 40, :] = first * turn_sin + second * turn_cos

    def turn_factors():
        raw_t[...] = raw[...].T
        for g in range(groups):
            for r in range(row_count):
                start = r * groups * span + g * span
                raw_p[g * slab + r * span : g * slab + (r + 1) * span, :] = raw_t[start : start + span, :]
        factors(0, raw_p[...].T)
        factors(1, raw[...])

    def mixing():
        edge = row_count * span
        position = jnp.concatenate([info[s, 0 : 2 * span, :] for s in range(J)], axis=0)
        position = jnp.concatenate([position] * (edge // 128), axis=1) if edge > 128 else position
        sub = lax.broadcasted_iota(jnp.int32, (edge, edge), 0)
        lane = lax.broadcasted_iota(jnp.int32, (edge, edge), 1)
        before, now = jnp.ones_like(position), position
        chosen = jnp.where(lane // span == 0, before, jnp.where(lane // span == 1, now, 0.0))
        for order in range(1, ring - 1):
            before, now = now, ((2.0 * order + 1.0) * position * now - order * before) / (order + 1.0)
            chosen = jnp.where(lane // span == order + 1, now, chosen)
        chosen = jnp.where(sub % span == lane % span, chosen, 0.0)
        mix[...] = chosen.astype(jnp.bfloat16)
        mix_t[...] = chosen.T.astype(jnp.bfloat16)

    def index_of(band):
        return (band // plane_count) * 8 + band % plane_count

    def build_lanes(band, carry):
        index = index_of(band)
        cf_re, cf_im = fac[pl.ds(64 + index, 1), :], fac[pl.ds(96 + index, 1), :]
        rf_re, rf_im = fac[pl.ds(index, 1), :], fac[pl.ds(32 + index, 1), :]
        col_base, row_base = pl.multiple_of(band * M, M), pl.multiple_of(band * 2 * M, 2 * M)
        for m in range(0, M, 16):
            ker_re, ker_im = ker_t[0, 0, m : m + 16, :], ker_t[0, 1, m : m + 16, :]
            col_t[pl.ds(col_base + m, 16), 0:size] = (cf_re * ker_re - cf_im * ker_im).astype(jnp.bfloat16)
            col_t[pl.ds(col_base + m, 16), size : 2 * size] = (cf_re * ker_im + cf_im * ker_re).astype(jnp.bfloat16)
            ker_re, ker_im = ker_t[1, 0, m : m + 16, :], ker_t[1, 1, m : m + 16, :]
            row_t[pl.ds(row_base + m, 16), :] = (rf_re * ker_re - rf_im * ker_im).astype(jnp.bfloat16)
            row_t[pl.ds(row_base + M + m, 16), :] = (rf_re * ker_im + rf_im * ker_re).astype(jnp.bfloat16)
        return carry

    def build_sublanes(axis, held, table):
        def step(i, carry):
            at = pl.ds(pl.multiple_of(i * 32, 32), 32)
            ker_re, ker_im = ker_n[1 - axis, 0, at, :], ker_n[1 - axis, 1, at, :]
            values = held[at, :]
            turned = []
            for p in range(plane_count):
                turn_cos, turn_sin = values[:, p : p + 1], values[:, 8 + p : 9 + p]
                turned.append((turn_cos * ker_re - turn_sin * ker_im, turn_cos * ker_im + turn_sin * ker_re))
            for q in range(src_count):
                start = 16 + 32 * axis + 8 * q
                first = jnp.broadcast_to(values[:, start : start + 1], (32, M))
                second = jnp.broadcast_to(values[:, start + 1 : start + 2], (32, M))
                for p, (real, imag) in enumerate(turned):
                    band = q * plane_count + p
                    table[band, at, 0:M] = (first * real - second * imag).astype(jnp.bfloat16)
                    table[band, at, M : 2 * M] = (first * imag + second * real).astype(jnp.bfloat16)
            return carry

        return step

    build_col = build_sublanes(1, raw_t, col_n)
    build_row = build_sublanes(0, raw_p, row_n)
    slices = size // 32

    def start_tables():
        phases()
        turn_factors()
        mixing()
        for load in loads[4:6]:
            load.wait()

    def own(g):
        for way in range(2):
            gather_send(way, g, 0)

    def second(g):
        up = long_way(g)
        gather_arrived(up, g, 1)
        gather_send(up, g, 1, 2)
        gather_send(up, g, 1)
        gather_arrived(1 - up, g, 1)
        gather_send(1 - up, g, 1)

    def third(g):
        up = long_way(g)
        gather_arrived(up, g, 3)
        gather_send(up, g, 3)
        gather_arrived(1 - up, g, 2)
        gather_send(1 - up, g, 2)

    def gathered(g):
        up = long_way(g)
        gather_arrived(up, g, 2)
        gather_arrived(up, g, 4)
        gather_arrived(1 - up, g, 3)

    def masked(values, g):
        mask = support[g * span : (g + 1) * span, :].astype(jnp.float32)
        mask = jnp.concatenate([mask, mask], axis=1)
        return values * jnp.concatenate([mask] * (values.shape[0] // span), axis=0)

    def pupils(g):
        gathered(g)
        summed = jnp.dot(mix[...], coeff[group(g), :], preferred_element_type=jnp.float32)
        pupil_out[group(g), :] = masked(summed, g).astype(jnp.bfloat16)
        for d, peer in enumerate(peers):
            send(
                pupil_out.at[rows_of(peer, g), :], pupil_in.at[rows_of(me_r, g), :],
                out_send.at[0], out_recv.at[g], (me_f, peer),
            )
        pupil_in[rows_of(me_r, g), :] = pupil_out[rows_of(me_r, g), :]

    def on_core(core, what):
        pl.when(j % 2 == core)(what)

    def build(step, *parts):
        (start0, stop0), (start1, stop1) = parts
        first = jnp.where(j % 2 == 0, start0, start1)
        lax.fori_loop(first, jnp.where(j % 2 == 0, stop0, stop1), step, 0)

    def own_blocks():
        for g in range(groups):
            own(g)

    def second_step():
        for g in range(groups):
            second(g)

    on_core(1, own_blocks)
    for d, device in enumerate(siblings):
        send(info.at[j], info.at[j], info_send.at[0], info_recv.at[d], device)
    windows()
    on_core(0, own_blocks)
    on_core(1, second_step)
    for d in range(J - 1):
        arrived(info.at[(j + J - 1 - d) % J], info_send.at[0], info_recv.at[d], siblings[d])
    start_tables()
    loads[1].wait()
    on_core(0, second_step)
    build(build_lanes, (0, bands // 2), (0, 0))
    build(build_row, (0, slices // 2), (0, 0))
    build(build_col, (0, slices // 2), (0, slices // 2))
    for g in range(groups):
        third(g)
        build(build_row, (0, 0), (g * slices // 8, (g + 1) * slices // 8))
    build(build_col, (slices // 2, slices), (slices // 2, 5 * slices // 8))
    for g in range(groups):
        pupils(g)
    build(build_col, (0, 0), (5 * slices // 8, slices))
    build(build_lanes, (bands // 2, bands), (0, bands))
    build(build_row, (slices // 2, slices), (0, 0))

    def exchanged(landed, send_sem, recv_sem, g):
        blocks = landed.at[g * slab : g * slab + len(peers) * span, :]
        arrived(blocks, send_sem.at[0], recv_sem.at[g], (me_f, peers[0]))

    def spectra_of(g, band):
        stacked = jnp.concatenate([pupil_in[group(g), 0:size], pupil_in[group(g), size : 2 * size]], axis=0)
        prod = jnp.dot(stacked, col_n[band], preferred_element_type=jnp.float32)
        real = prod[:slab, :M] - prod[slab:, M:]
        imag = prod[:slab, M:] + prod[slab:, :M]
        return jnp.concatenate([real, imag], axis=1).astype(jnp.bfloat16)

    def spectra(g):
        exchanged(pupil_in, out_send, out_recv, g)

        def step(band, carry):
            spec[band, g % 2 * slab : (g % 2 + 1) * slab, :] = spectra_of(g, band)
            return carry

        lax.fori_loop(0, bands, step, 0, unroll=True)

    def images(g):
        def step(band, carry):
            base = pl.multiple_of(band * 2 * M, 2 * M)
            kernel = row_t[pl.ds(base, 2 * M), g * slab : (g + 2) * slab]
            term = jnp.dot(kernel, spec[band], preferred_element_type=jnp.float32)
            image[band] = term if g == 0 else image[band] + term
            return carry

        lax.fori_loop(0, bands, step, 0, unroll=True)

    def adjoints():
        def step(band, carry):
            term = image[band]
            weight = weights[band]
            real = (weight * (term[:M, :M] - term[M:, M:])).astype(jnp.bfloat16)
            imag = (weight * (term[:M, M:] + term[M:, :M])).astype(jnp.bfloat16)
            square = jnp.concatenate(
                [jnp.concatenate([real, imag], axis=1), jnp.concatenate([imag, -real], axis=1)], axis=0
            )
            back = jnp.dot(row_n[band], square, preferred_element_type=jnp.float32).astype(jnp.bfloat16)
            at = pl.ds(pl.multiple_of(band * M, M), M)
            adj_re[:, at] = back[:, :M]
            adj_im[:, at] = back[:, M:]
            return carry

        lax.fori_loop(0, bands, step, 0, unroll=True)

    loads[6].wait()
    spectra(0)
    spectra(1)
    images(0)
    build(build_row, (0, 0), (slices // 2, slices))
    spectra(2)
    spectra(3)
    images(2)
    adjoints()

    def pull(g):
        rows = slice(g * slab, (g + 1) * slab)
        stacked = jnp.concatenate([adj_re[rows, :], adj_im[rows, :]], axis=0)
        with_re = jnp.dot(stacked, col_t[:, 0:size], preferred_element_type=jnp.float32)
        with_im = jnp.dot(stacked, col_t[:, size : 2 * size], preferred_element_type=jnp.float32)
        pulled[group(g), 0:size] = (with_re[:slab] + with_im[slab:]).astype(jnp.bfloat16)
        pulled[group(g), size : 2 * size] = (with_re[slab:] - with_im[:slab]).astype(jnp.bfloat16)
        for d, peer in enumerate(peers):
            send(
                pulled.at[rows_of(peer, g), :], returned.at[rows_of(me_r, g), :],
                back_send.at[0], back_recv.at[g], (me_f, peer),
            )
        returned[rows_of(me_r, g), :] = pulled[rows_of(me_r, g), :]

    def scatter_slot(g, k):
        return part_in.at[g, rows_of(k), :]

    def coded(values):
        top = jnp.max(jnp.abs(values), axis=1, keepdims=True)
        power = jnp.ceil(jnp.log2(jnp.maximum(jnp.broadcast_to(top, (span, 128)), 2.0**-120)))
        scale = jnp.concatenate([jnp.exp2(-power)] * (2 * size // 128), axis=1)
        levels = jnp.round(values * scale * LEVELS)
        return levels.astype(jnp.int32).astype(jnp.int16), power.astype(jnp.int32).astype(jnp.int16)

    def decoded(slot):
        power = slot[:, 2 * size :].astype(jnp.int32).astype(jnp.float32)
        scale = jnp.concatenate([jnp.exp2(power) * (1.0 / LEVELS)] * (2 * size // 128), axis=1)
        return slot[:, 0 : 2 * size].astype(jnp.int32).astype(jnp.float32) * scale

    def scatter_send(g, k, slot, arrival, device):
        levels, power = coded(part[rows_of(k, g), :])
        part_out[rows_of(k, g), 0 : 2 * size] = levels
        part_out[rows_of(k, g), 2 * size :] = power
        send(part_out.at[rows_of(k, g), :], scatter_slot(g, slot), rs_send.at[0], rs_recv.at[g, arrival], device)

    def scatter_arrived(g, slot, arrival):
        arrived(scatter_slot(g, slot), rs_send.at[0], rs_recv.at[g, arrival], right)
        return decoded(scatter_slot(g, slot))

    def take_in(g, k, slot, arrival):
        part[rows_of(k, g), :] = part[rows_of(k, g), :] + scatter_arrived(g, slot, arrival)

    def collect(g):
        up = long_way(g)
        exchanged(returned, back_send, back_recv, g)
        part[group(g), :] = jnp.dot(mix_t[...], returned[group(g), :], preferred_element_type=jnp.float32)
        scatter_send(g, ahead(up, 4), ahead(up, 4), 0, ring_to(up))
        scatter_send(g, ahead(1 - up, 3), ahead(1 - up, 3), 1, ring_to(1 - up))

        def more():
            scatter_send(g, ahead(up, 2), ahead(up, 2), 2, ring_to(up))
            if g >= groups // 2:
                scatter_send(g, ahead(1 - up, 1), ring, 3, ring_to(1 - up))

        on_core(0, more)

    def pass_on(g, way, n, arrival, slot, next_arrival):
        k = ahead(way, n)
        take_in(g, k, k, arrival)
        scatter_send(g, k, k if slot is None else slot, next_arrival, ring_to(way))

    def combine_two(g):
        up = long_way(g)
        for way, n, arrival, slot in ((up, 3, 0, ring + 2), (1 - up, 2, 1, ring + 1), (up, 1, 2, None)):
            k = ahead(way, n)
            take_in(g, k, k, arrival)
            scatter_send(g, k, k if slot is None else slot, arrival + 4, ring_to(way, n))

    def combine_three(g):
        up = long_way(g)
        far, near = ahead(up, 3), ahead(1 - up, 2)
        take_in(g, far, far, 0)
        scatter_send(g, far, ring + 2, 4, ring_to(up, 2))
        take_in(g, near, near, 1)
        scatter_send(g, near, near, 5, ring_to(1 - up))

    def deliver_three(g):
        up = long_way(g)
        first, other = ahead(up, 1), ahead(1 - up, 1)
        take_in(g, other, other, 5)
        scatter_send(g, other, ring, 3, ring_to(1 - up))
        take_in(g, first, first, 2)
        take_in(g, first, ring + 2, 4)
        scatter_send(g, first, first, 6, ring_to(up))

    def leave(g):
        return pltpu.make_async_copy(out.at[g], out_hbm.at[0, :, g * span : (g + 1) * span, :], out_sem.at[g])

    def finish(g, *arrivals):
        total = part[rows_of(z, g), :] + scatter_arrived(g, z, 6)
        for slot, arrival in arrivals:
            total = total + scatter_arrived(g, slot, arrival)
        total = masked(total, g)
        for c in range(2):
            out[g, c] = total[:, c * size : (c + 1) * size]
        leave(g).start()

    def with_jumps():
        for g in range(groups):
            (combine_three if g < groups // 2 else combine_two)(g)
        for g in range(groups // 2):
            deliver_three(g)
        for g in range(groups):
            finish(g, *[(ring, 3), (ring + 2, 4), (ring + 1, 5)][: 1 if g < groups // 2 else 3])

    def place_to_place():
        for g in range(groups):
            pass_on(g, long_way(g), 3, 0, None, 2)
            pass_on(g, 1 - long_way(g), 2, 1, None, 4)
        for g in range(groups):
            pass_on(g, long_way(g), 2, 2, None, 5)
            pass_on(g, 1 - long_way(g), 1, 4, ring, 3)
        for g in range(groups):
            pass_on(g, long_way(g), 1, 5, None, 6)
        for g in range(groups):
            finish(g, (ring, 3))

    for g in range(groups):
        pull(g)
    for g in range(groups):
        collect(g)
    on_core(0, with_jumps)
    on_core(1, place_to_place)

    rounds = (ring - 1) * groups * span
    for moved, count, sem in (
        (info, J - 1, info_send), (coeff, rounds, ag_send), (pupil_out, len(peers) * groups * span, out_send),
        (pulled, len(peers) * groups * span, back_send), (part_out, rounds, rs_send),
    ):
        all_sent = moved.at[0:count]
        pltpu.make_async_remote_copy(
            src_ref=all_sent, dst_ref=all_sent, send_sem=sem.at[0], recv_sem=sem.at[0], device_id=right, device_id_type=MESH
        ).wait_send()
    for g in range(groups):
        leave(g).wait()


def local(direction, slits, sources, support, focus, slit_focus, obj_rows, obj_cols, weights):
    row_count = lax.axis_size("row")
    ring = lax.axis_size("field") // J
    size = direction.shape[3]
    src_count, plane_count = sources.shape[0], focus.shape[0]
    bands = src_count * plane_count
    span = size // (row_count * GROUPS)
    slab = span * row_count
    total_slits = slits.shape[0] * lax.axis_size("field")
    ker_t, ker_n = kernel_tables(size, row_count, GROUPS)
    weights = weights.reshape(bands, M, M)
    smem = pl.BlockSpec(memory_space=pltpu.SMEM)
    hbm = pl.BlockSpec(memory_space=pl.ANY)
    dma = pltpu.SemaphoreType.DMA
    half = ring // 2
    peers = row_count - 1
    f32, bf16 = jnp.float32, jnp.bfloat16
    sums = pl.pallas_call(
        functools.partial(body, (ring, row_count, src_count, plane_count, size)),
        out_shape=jax.ShapeDtypeStruct(direction.shape, jnp.float32),
        in_specs=[smem] * 4 + [hbm] * 7,
        out_specs=hbm,
        scratch_shapes=[
            pltpu.VMEM(direction.shape, bf16),
            pltpu.VMEM(support.shape, jnp.int32),
            pltpu.VMEM(obj_rows.shape, f32),
            pltpu.VMEM(obj_cols.shape, f32),
            pltpu.VMEM(weights.shape, f32),
            pltpu.VMEM(ker_t.shape, f32),
            pltpu.VMEM(ker_n.shape, f32),
            pltpu.VMEM((J, 4 * span, 128), f32),
            pltpu.VMEM((GROUPS * ring * span, 2 * size), bf16),
            pltpu.VMEM((slab, ring * span), bf16),
            pltpu.VMEM((ring * span, slab), bf16),
            pltpu.VMEM((128, size), f32),
            pltpu.VMEM((size, 128), f32),
            pltpu.VMEM((size, 128), f32),
            pltpu.VMEM((128, size), f32),
            pltpu.VMEM((bands * M, 2 * size), bf16),
            pltpu.VMEM((bands * 2 * M, size), bf16),
            pltpu.VMEM((bands, size, 2 * M), bf16),
            pltpu.VMEM((bands, size, 2 * M), bf16),
            pltpu.VMEM((GROUPS * slab, 2 * size), bf16),
            pltpu.VMEM((GROUPS * slab, 2 * size), bf16),
            pltpu.VMEM((bands, 2 * slab, 2 * M), bf16),
            pltpu.VMEM((bands, 2 * M, 2 * M), f32),
            pltpu.VMEM((size, bands * M), bf16),
            pltpu.VMEM((size, bands * M), bf16),
            pltpu.VMEM((GROUPS * slab, 2 * size), bf16),
            pltpu.VMEM((GROUPS * slab, 2 * size), bf16),
            pltpu.VMEM((GROUPS * ring * span, 2 * size), f32),
            pltpu.VMEM((GROUPS * ring * span, 2 * size + 128), jnp.int16),
            pltpu.VMEM((GROUPS, (ring + 3) * span, 2 * size + 128), jnp.int16),
            pltpu.VMEM((GROUPS, 2, span, size), f32),
            dma((7,)),
            dma((GROUPS,)),
            dma((1,)),
            dma((J - 1,)),
            dma((1,)),
            dma((2, GROUPS, half)),
            dma((1,)),
            dma((GROUPS,)),
            dma((1,)),
            dma((GROUPS,)),
            dma((1,)),
            dma((GROUPS, ring - 1)),
        ],
        compiler_params=pltpu.CompilerParams(
            collective_id=0, has_side_effects=True, vmem_limit_bytes=56 * 1024 * 1024
        ),
    )(slits, sources, focus, slit_focus, direction, support, obj_rows, obj_cols, weights, ker_t, ker_n)
    return sums * (4.0 / (bands * total_slits))


def solution(mesh):
    return jax.shard_map(
        local,
        mesh=mesh,
        in_specs=(
            P("field", None, "row", None),
            P("field"),
            P(),
            P("row", None),
            P(),
            P("field"),
            P(),
            P(),
            P(),
        ),
        out_specs=P("field", None, "row", None),
        check_vma=False,
    )
```
